32 devices in a mesh: seq: 4 (over y, x), win: 8 (over z, core).
Axes of the slice: x: 2, y: 2, z: 4, core: 2. Of those that a mesh axis runs over, the one named last changes fastest.
Arguments:
- features: bfloat16 [8, 1536, 1536], P('win', 'seq'), may hold values from -24 to 24
- species: int32 [8], P('win'), may hold values 0 or 1
- crop_start: int32 [8], P('win'), may hold values from 0 to 640
- human_grad: bfloat16 [8, 1536, 5313], P('win', 'seq'), may hold values from -6 to 6
- mouse_grad: bfloat16 [8, 1536, 1643], P('win', 'seq'), may hold values from -6 to 6
- batch_gain: float32 [1536], replicated, may hold values from 0.1 to 1.9
- batch_bias: float32 [1536], replicated, may hold values from -1.5 to 1.5
- first_gain: float32 [1536], replicated, may hold values from 0.1 to 1.9
- first_bias: float32 [1536], replicated, may hold values from -1.5 to 1.5
- w_query: bfloat16 [1536, 512], P(('seq', 'win')), may hold values from -0.15625 to 0.15625
- w_key: bfloat16 [1536, 512], P(('seq', 'win')), may hold values from -0.15625 to 0.15625
- w_value: bfloat16 [1536, 1536], P(('seq', 'win')), may hold values from -0.15625 to 0.15625
- w_position: bfloat16 [192, 512], replicated, may hold values from -0.875 to 0.875
- content_bias: float32 [8, 64], replicated, may hold values from -0.5 to 0.5
- position_bias: float32 [8, 64], replicated, may hold values from -0.5 to 0.5
- w_out: bfloat16 [1536, 1536], P(('seq', 'win')), may hold values from -1.25 to 1.25
- b_out: float32 [1536], replicated, may hold values from -1.5 to 1.5
- second_gain: float32 [1536], replicated, may hold values from 0.1 to 1.9
- second_bias: float32 [1536], replicated, may hold values from -1.5 to 1.5
- w_up: bfloat16 [1536, 3072], P(('seq', 'win')), may hold values from -0.15625 to 0.15625
- b_up: float32 [3072], replicated, may hold values from -2.5 to 2.5
- w_down: bfloat16 [3072, 1536], P(('seq', 'win')), may hold values from -0.109375 to 0.109375
- b_down: float32 [1536], replicated, may hold values from -1.5 to 1.5
- w_human: bfloat16 [1536, 5313], P(('seq', 'win')), may hold values from -0.15625 to 0.15625
- b_human: float32 [5313], replicated, may hold values from -4 to 4
- w_mouse: bfloat16 [1536, 1643], P(('seq', 'win')), may hold values from -0.15625 to 0.15625
- b_mouse: float32 [1643], replicated, may hold values from -4 to 4
Outputs:
- layer_out: bfloat16 [8, 1536, 1536], P('win', 'seq')
- input_grad: bfloat16 [8, 1536, 1536], P('win', 'seq')
- grad_batch_gain: float32 [1536], replicated
- grad_batch_bias: float32 [1536], replicated
- grad_first_gain: float32 [1536], replicated
- grad_first_bias: float32 [1536], replicated
- grad_query: float32 [1536, 512], P(('seq', 'win'))
- grad_key: float32 [1536, 512], P(('seq', 'win'))
- grad_value: float32 [1536, 1536], P(('seq', 'win'))
- grad_position: float32 [192, 512], replicated
- grad_content_bias: float32 [8, 64], replicated
- grad_position_bias: float32 [8, 64], replicated
- grad_out: float32 [1536, 1536], P(('seq', 'win'))
- grad_out_bias: float32 [1536], replicated
- grad_second_gain: float32 [1536], replicated
- grad_second_bias: float32 [1536], replicated
- grad_up: float32 [1536, 3072], P(('seq', 'win'))
- grad_up_bias: float32 [3072], replicated
- grad_down: float32 [3072, 1536], P(('seq', 'win'))
- grad_down_bias: float32 [1536], replicated
- grad_human: float32 [1536, 5313], P(('seq', 'win'))
- grad_human_bias: float32 [5313], replicated
- grad_mouse: float32 [1536, 1643], P(('seq', 'win'))
- grad_mouse_bias: float32 [1643], replicated
The draws below stay inside these ranges and needn't reach their ends.
Inputs may be any that keep to these rules, and one draw needn't show every extreme that they name: `species`: 1 marks a mouse window, 0 a human one. `crop_start`: the scored bins of a window are the 896 bins from this offset.
All inputs are finite; a program needn't handle non-finite values. No bound on the sum of `species` on one device may be relied on, other than what follows from the above.
Results may differ from the reference program's by a relative error of at most 0.018.
Values may be sent and summed in bfloat16 or wider, within the bound.
No kernel may reach another device: no remote copies, remote signals or barrier semaphores. Data moves between devices by JAX's collectives and lax.ppermute only.
A program may use at most 320 MiB of HBM per device.

```python
import math
import jax
import jax.numpy as jnp
from jax import lax

D = 1536
HEADS = 8
QK = 64
VH = 192
FF = 3072
TRACKS_HUMAN = 5313
TRACKS_MOUSE = 1643
RELF = 192
LEN = 1536
CROP = 896
WINDOWS = 8


def draw_features(key, part):
    key = jax.random.fold_in(key, 7)
    base_key, shift_key = jax.random.split(key, 2)
    full_shape = (WINDOWS, LEN, D)
    window_frac = jnp.arange(WINDOWS).astype(jnp.float32).reshape(WINDOWS, 1, 1) / max(WINDOWS - 1, 1)
    bin_frac = jnp.arange(LEN).astype(jnp.float32).reshape(1, LEN, 1) / max(LEN - 1, 1)
    growth = 1.0 + window_frac + bin_frac
    offsets = 0.5 * jnp.clip(jax.random.normal(shift_key, (D,), jnp.float32), -2.0, 2.0)
    values_base = jnp.clip(jax.random.normal(base_key, full_shape, jnp.float32), -4.0, 4.0)
    return (values_base * growth + offsets).astype(jnp.bfloat16)


def touch_ends(entries, rng, smallest, largest):
    longest = entries.shape.index(max(entries.shape))
    spots = []
    for shift in (0, 1):
        where = [jax.random.randint(jax.random.fold_in(rng, axis), (), 0, length) for axis, length in enumerate(entries.shape)]
        where[longest] = (where[longest] + shift) % entries.shape[longest]
        spots.append(tuple(where))
    return entries.at[spots[0]].set(smallest).at[spots[1]].set(largest)


def level_of(rng, shape, shards, low, largest):
    def one(position, shards_of):
        draws = jax.random.uniform(jax.random.fold_in(jax.random.fold_in(rng, 6), position), (shards_of,), jnp.float32, low / len(shards), largest / len(shards))
        return jnp.repeat(jnp.exp(draws), shape[position] // shards_of).reshape((-1,) + (1,) * (len(shape) - position - 1))

    level = one(*shards[0])
    for cut in shards[1:]:
        level = level * one(*cut)
    return level


def bell_draw(rng, dims, scale, most, cuts=(), held_as=jnp.bfloat16):
    level = level_of(rng, dims, cuts, -0.22, 0.18) if cuts else 1.0
    array = jax.random.normal(rng, dims, jnp.float32) * scale * level
    return jnp.minimum(jnp.maximum(array, -most), most).astype(held_as)


def setup_inputs(seed: int = 0) -> dict:
    arg_keys = jax.random.split(jax.random.key(seed), 28)
    features = draw_features(jax.random.fold_in(arg_keys[27], 71), 0)
    species = touch_ends((jax.random.randint(arg_keys[1], (WINDOWS,), 0, 3) < 1).astype(jnp.int32), jax.random.fold_in(arg_keys[1], 1), 0, 1)
    crop_start = touch_ends(jax.random.randint(arg_keys[2], (WINDOWS,), 0, LEN - CROP + 1), jax.random.fold_in(arg_keys[2], 1), 0, LEN - CROP).astype(jnp.int32)
    human_grad = bell_draw(arg_keys[3], (WINDOWS, LEN, TRACKS_HUMAN), 1.0, 6.0, ((0, 8), (1, 4)))
    mouse_grad = bell_draw(arg_keys[4], (WINDOWS, LEN, TRACKS_MOUSE), 1.0, 6.0, ((0, 8), (1, 4)))
    batch_gain = jnp.clip(1.0 + 0.18 * jax.random.normal(arg_keys[5], (D,), jnp.float32), 0.1, 1.9)
    batch_bias = bell_draw(arg_keys[6], (D,), 0.3, 1.5, (), jnp.float32)
    first_gain = jnp.clip(1.0 + 0.18 * jax.random.normal(arg_keys[7], (D,), jnp.float32), 0.1, 1.9)
    first_bias = bell_draw(arg_keys[8], (D,), 0.3, 1.5, (), jnp.float32)
    w_query = bell_draw(arg_keys[9], (D, HEADS * QK), D ** -0.5, 0.15625, ((0, 32),))
    w_key = bell_draw(arg_keys[10], (D, HEADS * QK), D ** -0.5, 0.15625, ((0, 32),))
    w_value = bell_draw(arg_keys[11], (D, D), D ** -0.5, 0.15625, ((0, 32),))
    w_position = bell_draw(arg_keys[12], (RELF, HEADS * QK), (RELF // 4) ** -0.5, 0.875)
    content_bias = bell_draw(arg_keys[13], (HEADS, QK), 0.1, 0.5, (), jnp.float32)
    position_bias = bell_draw(arg_keys[14], (HEADS, QK), 0.1, 0.5, (), jnp.float32)
    w_out = bell_draw(arg_keys[15], (D, D), (D // 64) ** -0.5, 1.25, ((0, 32),))
    b_out = bell_draw(arg_keys[16], (D,), 0.3, 1.5, (), jnp.float32)
    second_gain = jnp.clip(1.0 + 0.18 * jax.random.normal(arg_keys[17], (D,), jnp.float32), 0.1, 1.9)
    second_bias = bell_draw(arg_keys[18], (D,), 0.3, 1.5, (), jnp.float32)
    w_up = bell_draw(arg_keys[19], (D, FF), D ** -0.5, 0.15625, ((0, 32),))
    b_up = bell_draw(arg_keys[20], (FF,), 0.5, 2.5, (), jnp.float32)
    w_down = bell_draw(arg_keys[21], (FF, D), FF ** -0.5, 0.109375, ((0, 32),))
    b_down = bell_draw(arg_keys[22], (D,), 0.3, 1.5, (), jnp.float32)
    w_human = bell_draw(arg_keys[23], (D, TRACKS_HUMAN), D ** -0.5, 0.15625, ((0, 32),))
    b_human = bell_draw(arg_keys[24], (TRACKS_HUMAN,), 1.0, 4.0, (), jnp.float32)
    w_mouse = bell_draw(arg_keys[25], (D, TRACKS_MOUSE), D ** -0.5, 0.15625, ((0, 32),))
    b_mouse = bell_draw(arg_keys[26], (TRACKS_MOUSE,), 1.0, 4.0, (), jnp.float32)
    return dict(features=features, species=species, crop_start=crop_start, human_grad=human_grad, mouse_grad=mouse_grad, batch_gain=batch_gain, batch_bias=batch_bias, first_gain=first_gain, first_bias=first_bias, w_query=w_query, w_key=w_key, w_value=w_value, w_position=w_position, content_bias=content_bias, position_bias=position_bias, w_out=w_out, b_out=b_out, second_gain=second_gain, second_bias=second_bias, w_up=w_up, b_up=b_up, w_down=w_down, b_down=b_down, w_human=w_human, b_human=b_human, w_mouse=w_mouse, b_mouse=b_mouse)


@jax.custom_vjp
def low(v):
    return lax.optimization_barrier(v.astype(jnp.bfloat16)).astype(jnp.float32)

@jax.custom_vjp
def low_back(v):
    return v

def low_keep(v):
    return (low(v), None)

def low_pass(kept, grad):
    return (grad,)

def back_keep(v):
    return (v, None)

def back_low(kept, grad):
    return (low(grad),)
low.defvjp(low_keep, low_pass)
low_back.defvjp(back_keep, back_low)
HIGHEST = lax.Precision.HIGHEST

def matmul(left, right):
    return jnp.dot(left, right, precision=HIGHEST, preferred_element_type=jnp.float32)

def position_basis(distance, feature_count, window_length):
    per_kind = feature_count // 6
    magnitude = jnp.abs(distance)[:, None]
    kind_index = jnp.arange(per_kind).astype(jnp.float32)[None, :]
    top_log = math.log2(window_length)
    half_life = 2.0 ** (3.0 + (top_log - 3.0) * kind_index / max(per_kind - 1, 1))
    decays = jnp.exp(-math.log(2.0) * magnitude / half_life)
    widths = 2.0 ** (kind_index + 1.0) - 1.0
    central = jnp.where(widths > magnitude, 1.0, 0.0).astype(jnp.float32)
    centers = window_length * kind_index / per_kind
    spread = window_length / per_kind
    bumps = jnp.exp(-0.5 * ((magnitude - centers) / spread) ** 2)
    even_part = jnp.concatenate([decays, central, bumps], axis=1)
    return jnp.concatenate([even_part, jnp.sign(distance)[:, None] * even_part], axis=1)

def shift_rows(wide_scores, keep):
    lead = wide_scores.shape[:-2]
    row_count = wide_scores.shape[-2]
    col_count = wide_scores.shape[-1]
    padded = jnp.pad(wide_scores, [(0, 0)] * len(lead) + [(0, 0), (1, 0)])
    flat = padded.reshape(lead + (row_count * (col_count + 1),))[..., row_count:]
    return flat.reshape(lead + (row_count, col_count))[..., :keep]

def layer_norm(values, gain, bias):
    centered = values - lax.optimization_barrier(jnp.mean(values, -1, keepdims=True))
    variance = lax.optimization_barrier(jnp.mean(centered * centered, -1, keepdims=True))
    return centered * lax.rsqrt(variance + 1e-05) * gain + bias

def gelu_sigmoid(values):
    return values * jax.nn.sigmoid(1.702 * values)

def softplus(values):
    return jnp.maximum(values, 0.0) + jnp.log1p(jnp.exp(-jnp.abs(values)))

def reference(features, species, crop_start, human_grad, mouse_grad, batch_gain, batch_bias, first_gain, first_bias, w_query, w_key, w_value, w_position, content_bias, position_bias, w_out, b_out, second_gain, second_bias, w_up, b_up, w_down, b_down, w_human, b_human, w_mouse, b_mouse):
    params = tuple((param.astype(jnp.float32) for param in (batch_gain, batch_bias, first_gain, first_bias, w_query, w_key, w_value, w_position, content_bias, position_bias, w_out, b_out, second_gain, second_bias, w_up, b_up, w_down, b_down, w_human, b_human, w_mouse, b_mouse)))
    key_scale = QK ** (-0.5)
    inputs_f = features.astype(jnp.float32)
    positions = jnp.arange(LEN)

    def forward(inputs_in, params_in):
        g_batch, b_batch, g_first, b_first, p_query, p_key, p_value, p_position, c_bias, r_bias, p_out, o_bias, g_second, b_second, p_up, u_bias, p_down, d_bias, p_human, h_bias, p_mouse, m_bias = params_in
        channel_mean = lax.optimization_barrier(jnp.mean(inputs_in, axis=(0, 1)))
        square_mean = lax.optimization_barrier(jnp.mean(inputs_in * inputs_in, axis=(0, 1)))
        inv_std = lax.rsqrt(square_mean - channel_mean * channel_mean + 1e-05)
        normed = (inputs_in - channel_mean) * inv_std * g_batch + b_batch
        distance = (jnp.arange(2 * LEN - 1) - (LEN - 1)).astype(jnp.float32)
        rel_keys = low(matmul(low(position_basis(distance, RELF, LEN)), p_position)).reshape(2 * LEN - 1, HEADS, QK)

        def one_window(items):
            rows_in, human_cot, mouse_cot, kind, start = items
            attn_in = low(layer_norm(rows_in, g_first, b_first))
            queries = low_back(matmul(attn_in, p_query)).reshape(LEN, HEADS, QK) * key_scale
            q_content = low(queries + c_bias)
            q_position = low(queries + r_bias)
            keys = low(low_back(matmul(attn_in, p_key))).reshape(LEN, HEADS, QK)
            values = low(low_back(matmul(attn_in, p_value))).reshape(LEN, HEADS, VH)
            content = jnp.einsum('ihe,jhe->hij', q_content, keys, precision=HIGHEST)
            relative = jnp.einsum('ihe,mhe->him', q_position, rel_keys, precision=HIGHEST)
            scores = low_back(content + shift_rows(relative, LEN))
            top = lax.optimization_barrier(jnp.max(scores, -1, keepdims=True))
            expo = jnp.exp(scores - top)
            probs = expo / lax.optimization_barrier(jnp.sum(expo, -1, keepdims=True))
            mixed = jnp.einsum('hij,jhf->ihf', low(probs), values, precision=HIGHEST).reshape(LEN, D)
            attended = low(low_back(mixed))
            resid = rows_in + low_back(matmul(attended, p_out) + o_bias)
            mlp_in = low(layer_norm(resid, g_second, b_second))
            hidden = low_back(matmul(mlp_in, p_up) + u_bias)
            middle = low(gelu_sigmoid(hidden))
            layer = resid + low_back(matmul(middle, p_down) + d_bias)
            head_in = low(layer)
            inside = (positions >= start) & (positions < start + CROP)
            human_mask = (inside & (kind == 0)).astype(jnp.float32)[:, None]
            mouse_mask = (inside & (kind == 1)).astype(jnp.float32)[:, None]
            human_logit = low_back(matmul(head_in, p_human) + h_bias)
            mouse_logit = low_back(matmul(head_in, p_mouse) + m_bias)
            human_loss = jnp.sum(human_mask * human_cot.astype(jnp.float32) * softplus(human_logit))
            mouse_loss = jnp.sum(mouse_mask * mouse_cot.astype(jnp.float32) * softplus(mouse_logit))
            return (human_loss + mouse_loss, head_in)
        losses, outputs = lax.map(jax.checkpoint(one_window), (normed, human_grad, mouse_grad, species, crop_start))
        return (jnp.sum(losses), outputs)
    loss, pullback, outputs = jax.vjp(forward, inputs_f, params, has_aux=True)
    grad_inputs, grad_params = pullback(jnp.ones_like(loss))
    g_batch_gain, g_batch_bias, g_first_gain, g_first_bias, g_query, g_key, g_value, g_position, g_content, g_posbias, g_out, g_out_bias, g_second_gain, g_second_bias, g_up, g_up_bias, g_down, g_down_bias, g_human, g_human_bias, g_mouse, g_mouse_bias = grad_params
    return (outputs.astype(jnp.bfloat16), grad_inputs.astype(jnp.bfloat16), g_batch_gain, g_batch_bias, g_first_gain, g_first_bias, g_query, g_key, g_value, g_position, g_content, g_posbias, g_out, g_out_bias, g_second_gain, g_second_bias, g_up, g_up_bias, g_down, g_down_bias, g_human, g_human_bias, g_mouse, g_mouse_bias)
```

```python
import functools
import math

import jax
import jax.numpy as jnp
from jax import lax
from jax.experimental import pallas as pl
from jax.experimental.pallas import tpu as pltpu
from jax.sharding import PartitionSpec as P

CROP = 896


def position_basis(distance, feature_count, window_length):
    per_kind = feature_count // 6
    magnitude = jnp.abs(distance)[:, None]
    kind_index = jnp.arange(per_kind).astype(jnp.float32)[None, :]
    top_log = math.log2(window_length)
    half_life = 2.0 ** (3.0 + (top_log - 3.0) * kind_index / max(per_kind - 1, 1))
    decays = jnp.exp(-math.log(2.0) * magnitude / half_life)
    widths = 2.0 ** (kind_index + 1.0) - 1.0
    central = jnp.where(widths > magnitude, 1.0, 0.0).astype(jnp.float32)
    centers = window_length * kind_index / per_kind
    spread = window_length / per_kind
    bumps = jnp.exp(-0.5 * ((magnitude - centers) / spread) ** 2)
    even_part = jnp.concatenate([decays, central, bumps], axis=1)
    return jnp.concatenate([even_part, jnp.sign(distance)[:, None] * even_part], axis=1)


def norm_parts(values):
    centered = values - jnp.mean(values, -1, keepdims=True)
    inv_scale = lax.rsqrt(jnp.mean(centered * centered, -1, keepdims=True) + 1e-05)
    return (centered * inv_scale, inv_scale)


def norm_back(outer_grad, inner_grad, normed_hat, inv_scale, gain):
    scaled = inner_grad * gain
    gain_grad = jnp.sum(inner_grad * normed_hat, 0)
    bias_grad = jnp.sum(inner_grad, 0)
    total_grad = outer_grad + inv_scale * (
        scaled
        - jnp.mean(scaled, -1, keepdims=True)
        - normed_hat * jnp.mean(scaled * normed_hat, -1, keepdims=True)
    )
    return (total_grad, gain_grad, bias_grad)


def matmul(left, right):
    return jnp.dot(left, right, preferred_element_type=jnp.float32)


def xor_pairs(count, bit):
    return [(i, i ^ bit) for i in range(count)]


def bits_of(count):
    return [1 << i for i in range(count.bit_length() - 1)]


class Place:
    def __init__(self):
        self.seq_count = lax.axis_size("seq")
        self.win_count = lax.axis_size("win")
        self.seq = lax.axis_index("seq")
        win = lax.axis_index("win")
        self.core = win % 2
        self.ring = self.win_count // 2
        self.chip = win // 2

    def other_core(self, value):
        return lax.ppermute(value, "win", xor_pairs(self.win_count, 1))

    def next_chip(self, value):
        count = self.win_count
        return lax.ppermute(value, "win", [(i, (i + 2) % count) for i in range(count)])

    def across(self, value, bits):
        return lax.ppermute(value, "seq", xor_pairs(self.seq_count, bits))

    def total(self, value, over_seq=True):
        for bit in bits_of(self.win_count):
            value = value + lax.ppermute(value, "win", xor_pairs(self.win_count, bit))
        if over_seq:
            for bit in bits_of(self.seq_count):
                value = value + self.across(value, bit)
        return value

    def by_seq(self, blocks):
        for bit in bits_of(self.seq_count):
            flipped = (self.seq // bit) % 2 == 1
            blocks = [jnp.where(flipped, blocks[m ^ bit], b) for m, b in enumerate(blocks)]
        return blocks


def after(value, *earlier):
    return lax.optimization_barrier((value, *earlier))[0]


def gather_rows(place, shard, width):
    rows = shard.shape[0]
    ring, seq_count = place.ring, place.seq_count
    half = width // 2
    line = [shard]
    for _ in range(ring - 1):
        line.append(place.next_chip(line[-1]))
    last = line[-1]
    line = jnp.stack(line[::-1] + line[::-1])
    line = lax.dynamic_slice_in_dim(line, ring - 1 - place.chip, ring, 0)
    if seq_count == 4:
        one, two = place.across(line, 1), place.across(line, 2)
        blocks = [
            (0, 0, line),
            (1, 0, one),
            (2, 0, two),
            (3, 0, place.across(one[..., :half], 2)),
            (3, half, place.across(two[..., half:], 1)),
        ]
    else:
        blocks = [(0, 0, line)]
        for bit in bits_of(seq_count):
            blocks = blocks + [(m ^ bit, at, place.across(b, bit)) for m, at, b in blocks]
    whole = jnp.zeros((seq_count, ring, 2, rows, width), shard.dtype)
    for m, at, block in blocks:
        for side, piece in ((0, block), (1, place.other_core(block))):
            whole = lax.dynamic_update_slice(
                whole, piece[None, :, None], (place.seq ^ m, 0, place.core ^ side, 0, at)
            )
    return whole.reshape(seq_count * ring * 2 * rows, width), last


def add_low(left, right):
    return (left.astype(jnp.float32) + right.astype(jnp.float32)).astype(jnp.bfloat16)


def scatter_grad(place, inputs, deltas):
    rows = inputs.shape[1]
    width = deltas.shape[1]
    half, quarter = width // 2, width // 4
    seq_count, ring = place.seq_count, place.ring
    seq_rows = rows // seq_count
    low, high = deltas[:, :half], deltas[:, half:]
    mine = jnp.where(place.core == 0, low, high)
    theirs = jnp.where(place.core == 0, high, low)
    passed = place.other_core(matmul(inputs.T, theirs).astype(jnp.bfloat16))
    sums = (matmul(inputs.T, mine) + passed.astype(jnp.float32)).astype(jnp.bfloat16)
    sums = sums.reshape(seq_count, seq_rows, half)

    def block(m):
        return lax.dynamic_index_in_dim(sums, place.seq ^ m, 0, keepdims=False)

    if seq_count == 4:
        far = block(3)
        by_two = place.across(far[:, :quarter], 2)
        by_one = place.across(far[:, quarter:], 1)
        near = block(1)
        near = jnp.concatenate([add_low(near[:, :quarter], by_two), near[:, quarter:]], axis=1)
        next_ = block(2)
        next_ = jnp.concatenate([next_[:, :quarter], add_low(next_[:, quarter:], by_one)], axis=1)
        kept = [block(0), place.across(near, 1), place.across(next_, 2)]
    else:
        blocks = [block(m) for m in range(seq_count)]
        for bit in bits_of(seq_count)[::-1]:
            blocks = [add_low(blocks[m], place.across(blocks[m ^ bit], bit)) for m in range(bit)]
        kept = blocks
    kept = [k.reshape(ring, seq_rows // ring, half) for k in kept]

    def at(step):
        spot = (place.chip + 2 * ring - 1 - step) % ring
        return sum(
            lax.dynamic_index_in_dim(k, spot, 0, keepdims=False).astype(jnp.float32) for k in kept
        )

    running = at(0)
    for step in range(ring - 1):
        running = place.next_chip(running.astype(jnp.bfloat16)).astype(jnp.float32) + at(step + 1)
    own_rows = seq_rows // ring // 2
    upper, lower = running[:own_rows], running[own_rows:]
    passed = place.other_core(jnp.where(place.core == 0, lower, upper))
    own = jnp.where(place.core == 0, upper, lower)
    return jnp.where(
        place.core == 0,
        jnp.concatenate([own, passed], axis=1),
        jnp.concatenate([passed, own], axis=1),
    )


VMEM_LIMIT = 56 * 1024 * 1024


def up_to(value, step):
    return -(-value // step) * step


def dot_last(left, right):
    return lax.dot_general(left, right, (((1,), (1,)), ((), ())), preferred_element_type=jnp.float32)


def dot_plain(left, right):
    return jnp.dot(left, right, preferred_element_type=jnp.float32)


def head_lanes(head, width, total):
    return head * width // 128 * 128, min(up_to((head + 1) * width, 128), total)


def keep_lanes(block, first, low, high):
    lane = lax.broadcasted_iota(jnp.int32, block.shape, 1) + first
    return jnp.where((lane >= low) & (lane < high), block, jnp.zeros_like(block))


def window_width(length, bins):
    return up_to(length + bins + (0 if bins % 128 == 0 else 128), 128)


def window_start(length, bins, here):
    base = length - (here + 1) * bins
    if bins % 128 == 0:
        return pl.multiple_of(base, 128), 0
    start = pl.multiple_of(base // 128 * 128, 128)
    return start, base - start


def attend_kernel(sizes, where_ref, *refs):
    blocks, bins, heads, key_size, value_size, wide = sizes
    length = blocks * bins
    kw, vw = heads * key_size, heads * value_size
    pieces, rel_ref = refs[:blocks], refs[blocks]
    outs, probs_ref, keys, values = refs[blocks + 1 : 2 * blocks + 1], *refs[2 * blocks + 1 :]
    step = pl.program_id(0)
    place = where_ref[0]

    @pl.when(step == 0)
    def _():
        for m in range(blocks):
            rows = pl.ds(pl.multiple_of((place ^ m) * bins, bins), bins)
            keys[rows, :] = pieces[m][:, 2 * kw : 3 * kw]
            values[rows, :] = pieces[m][:, 3 * kw :]

    def one(m):
        here = place ^ m
        base, moved = window_start(length, bins, here)
        window = rel_ref[pl.ds(base, wide), :]
        for head in range(heads):
            low, high = head * key_size, (head + 1) * key_size
            q_content = keep_lanes(pieces[m][:, :kw], 0, low, high)
            q_position = keep_lanes(pieces[m][:, kw : 2 * kw], 0, low, high)
            relative = dot_last(q_position, window)
            relative = pltpu.roll(relative, wide - (bins - 1), 1, stride=1, stride_axis=0)
            if bins % 128:
                relative = pltpu.roll(relative, wide - moved, 1)
            scores = dot_last(q_content, keys[...]) + relative[:, :length]
            top = jnp.max(scores, -1, keepdims=True)
            expo = jnp.exp(scores - top)
            probs = (expo * (1.0 / jnp.sum(expo, -1, keepdims=True))).astype(jnp.bfloat16)
            probs_ref[0, head] = probs
            first, last = head_lanes(head, value_size, vw)
            mixed = dot_plain(probs, values[:, first:last])
            mixed = keep_lanes(mixed, first, head * value_size, (head + 1) * value_size)
            if head == 0:
                outs[m][...] = jnp.zeros_like(outs[m])
            outs[m][:, first:last] += mixed.astype(jnp.bfloat16)

    for m in range(blocks):
        pl.when(step == m)(functools.partial(one, m))


def attend(pieces, rel_keys, place, heads, key_size, value_size):
    blocks, bins = len(pieces), pieces[0].shape[0]
    length = blocks * bins
    wide = window_width(length, bins)
    kw, vw = heads * key_size, heads * value_size
    whole = lambda shape: pl.BlockSpec(shape, lambda i, *_: (0,) * len(shape))
    sizes = (blocks, bins, heads, key_size, value_size, wide)
    flops = 2 * heads * length * length * (2 * key_size + value_size)
    result = pl.pallas_call(
        functools.partial(attend_kernel, sizes),
        grid_spec=pltpu.PrefetchScalarGridSpec(
            num_scalar_prefetch=1,
            grid=(blocks,),
            in_specs=[whole(p.shape) for p in pieces] + [whole(rel_keys.shape)],
            out_specs=[whole((bins, vw))] * blocks
            + [pl.BlockSpec((1, heads, bins, length), lambda i, *_: (i, 0, 0, 0))],
            scratch_shapes=[
                pltpu.VMEM((length, kw), jnp.bfloat16),
                pltpu.VMEM((length, vw), jnp.bfloat16),
            ],
        ),
        out_shape=[jax.ShapeDtypeStruct((bins, vw), jnp.bfloat16)] * blocks
        + [jax.ShapeDtypeStruct((blocks, heads, bins, length), jnp.bfloat16)],
        compiler_params=pltpu.CompilerParams(vmem_limit_bytes=VMEM_LIMIT),
        cost_estimate=pl.CostEstimate(
            flops=flops * 2, bytes_accessed=2 * heads * length * length, transcendentals=heads * length * length
        ),
    )(place, *pieces, rel_keys)
    return result[:blocks], result[blocks]


def attend_back_kernel(sizes, where_ref, *refs):
    blocks, bins, heads, key_size, value_size, wide = sizes
    length = blocks * bins
    kw, vw = heads * key_size, heads * value_size
    key_scale = key_size ** (-0.5)
    pieces, grads, rel_ref, probs_ref = (
        refs[:blocks], refs[blocks : 2 * blocks], refs[2 * blocks], refs[2 * blocks + 1],
    )
    rest = refs[2 * blocks + 2 :]
    outs, rel_grad, sums, keys, values, key_grad, value_grad = rest[:blocks], *rest[blocks:]
    step = pl.program_id(0)
    place = where_ref[0]

    @pl.when(step == 0)
    def _():
        for m in range(blocks):
            rows = pl.ds(pl.multiple_of((place ^ m) * bins, bins), bins)
            keys[rows, :] = pieces[m][:, 2 * kw : 3 * kw]
            values[rows, :] = pieces[m][:, 3 * kw :]
        rel_grad[...] = jnp.zeros_like(rel_grad)
        sums[...] = jnp.zeros_like(sums)
        key_grad[...] = jnp.zeros_like(key_grad)
        value_grad[...] = jnp.zeros_like(value_grad)

    def one(m):
        here = place ^ m
        base, moved = window_start(length, bins, here)
        window = rel_ref[pl.ds(base, wide), :]
        total = None
        row = lax.broadcasted_iota(jnp.int32, (bins, bins), 0)
        col = lax.broadcasted_iota(jnp.int32, (bins, bins), 1)
        flip = jnp.where(row + col == bins - 1, 1.0, 0.0).astype(jnp.bfloat16)
        for head in range(heads):
            low, high = head * key_size, (head + 1) * key_size
            vlow, vhigh = head * value_size, (head + 1) * value_size
            first, last = head_lanes(head, value_size, vw)
            probs = probs_ref[0, head]
            out_grad = keep_lanes(grads[m][:, first:last], first, vlow, vhigh)
            prob_grad = dot_last(out_grad, values[:, first:last])
            probs_f = probs.astype(jnp.float32)
            row_delta = jnp.sum(probs_f * prob_grad, -1, keepdims=True)
            delta = (probs_f * (prob_grad - row_delta)).astype(jnp.bfloat16)
            value_grad[first:last, :] += dot_plain(out_grad.T, probs)
            q_content = keep_lanes(pieces[m][:, :kw], 0, low, high)
            q_position = keep_lanes(pieces[m][:, kw : 2 * kw], 0, low, high)
            key_grad[...] += dot_plain(q_content.T, delta)
            content = keep_lanes(dot_plain(delta, keys[...]), 0, low, high)
            shifted = jnp.concatenate(
                [dot_plain(flip, delta), jnp.zeros((bins, wide - length), jnp.float32)], axis=1
            )
            shifted = pltpu.roll(shifted, 0, 1, stride=1, stride_axis=0)
            if bins % 128:
                shifted = pltpu.roll(shifted, moved, 1)
            shifted = shifted.astype(jnp.bfloat16)
            position = keep_lanes(dot_plain(shifted, window), 0, low, high)
            position = jnp.dot(
                flip.astype(jnp.float32),
                position,
                precision=lax.Precision.HIGHEST,
                preferred_element_type=jnp.float32,
            )
            q_position = dot_plain(flip, q_position).astype(jnp.bfloat16)
            rel_grad[:, pl.ds(base, wide)] += dot_plain(q_position.T, shifted)
            sums[0:1, :] += jnp.sum(content, 0, keepdims=True)
            sums[1:2, :] += jnp.sum(position, 0, keepdims=True)
            both = content + position
            total = both if total is None else total + both
        outs[m][:, :kw] = (total * key_scale).astype(jnp.bfloat16)

    for m in range(blocks):
        pl.when(step == m)(functools.partial(one, m))

    @pl.when(step == blocks - 1)
    def _():
        keys[...] = key_grad[...].T.astype(jnp.bfloat16)
        values[...] = value_grad[...].T.astype(jnp.bfloat16)
        for m in range(blocks):
            rows = pl.ds(pl.multiple_of((place ^ m) * bins, bins), bins)
            outs[m][:, kw : 2 * kw] = keys[rows, :]
            outs[m][:, 2 * kw :] = values[rows, :]


def attend_back(pieces, grads, rel_keys, probs, place, heads, key_size, value_size):
    blocks, bins = len(pieces), pieces[0].shape[0]
    length = blocks * bins
    wide = window_width(length, bins)
    kw, vw = heads * key_size, heads * value_size
    whole = lambda shape: pl.BlockSpec(shape, lambda i, *_: (0,) * len(shape))
    sizes = (blocks, bins, heads, key_size, value_size, wide)
    rel_shape = (kw, rel_keys.shape[0])
    flops = 2 * heads * length * length * (4 * key_size + 2 * value_size)
    result = pl.pallas_call(
        functools.partial(attend_back_kernel, sizes),
        grid_spec=pltpu.PrefetchScalarGridSpec(
            num_scalar_prefetch=1,
            grid=(blocks,),
            in_specs=[whole(p.shape) for p in pieces]
            + [whole(g.shape) for g in grads]
            + [whole(rel_keys.shape)]
            + [pl.BlockSpec((1, heads, bins, length), lambda i, *_: (i, 0, 0, 0))],
            out_specs=[whole((bins, 2 * kw + vw))] * blocks + [whole(rel_shape), whole((8, kw))],
            scratch_shapes=[
                pltpu.VMEM((length, kw), jnp.bfloat16),
                pltpu.VMEM((length, vw), jnp.bfloat16),
                pltpu.VMEM((kw, length), jnp.float32),
                pltpu.VMEM((vw, length), jnp.float32),
            ],
        ),
        out_shape=[jax.ShapeDtypeStruct((bins, 2 * kw + vw), jnp.bfloat16)] * blocks
        + [jax.ShapeDtypeStruct(rel_shape, jnp.float32), jax.ShapeDtypeStruct((8, kw), jnp.float32)],
        compiler_params=pltpu.CompilerParams(vmem_limit_bytes=VMEM_LIMIT),
        cost_estimate=pl.CostEstimate(
            flops=flops * 2, bytes_accessed=2 * heads * length * length, transcendentals=0
        ),
    )(place, *pieces, *grads, rel_keys, probs)
    return result[:blocks], result[blocks], result[blocks + 1]


def shards(
    features,
    species,
    crop_start,
    human_grad,
    mouse_grad,
    batch_gain,
    batch_bias,
    first_gain,
    first_bias,
    w_query,
    w_key,
    w_value,
    w_position,
    content_bias,
    position_bias,
    w_out,
    b_out,
    second_gain,
    second_bias,
    w_up,
    b_up,
    w_down,
    b_down,
    w_human,
    b_human,
    w_mouse,
    b_mouse,
):
    place = Place()
    seq_count = place.seq_count
    windows, bin_count, model_width = features.shape
    assert windows == 1
    head_count, key_size = content_bias.shape
    value_size = model_width // head_count
    length = bin_count * seq_count
    token_total = bin_count * seq_count * place.win_count
    key_scale = key_size ** (-0.5)
    heads = head_count // seq_count
    kw, vw = heads * key_size, heads * value_size
    human_tracks, mouse_tracks = b_human.shape[0], b_mouse.shape[0]
    tracks = up_to(human_tracks + mouse_tracks, 1024)
    spare = tracks - human_tracks - mouse_tracks
    shard_rows = w_query.shape[0]
    attn_shard = jnp.concatenate(
        [
            w_query.reshape(shard_rows, seq_count, kw),
            w_key.reshape(shard_rows, seq_count, kw),
            w_value.reshape(shard_rows, seq_count, vw),
        ],
        axis=2,
    ).reshape(shard_rows, -1)
    head_shard = jnp.concatenate(
        [w_human, w_mouse, jnp.zeros((shard_rows, spare), jnp.bfloat16)], axis=1
    )
    head_full = lax.all_gather(head_shard, ("seq", "win"), axis=0, tiled=True)
    attn_full, sent = gather_rows(place, attn_shard, attn_shard.shape[1])
    out_full, sent = gather_rows(place, after(w_out, sent), w_out.shape[1])
    up_full, sent = gather_rows(place, after(w_up, sent), w_up.shape[1])
    down_full, sent = gather_rows(place, after(w_down, sent), w_down.shape[1])
    head_bias = jnp.concatenate([b_human, b_mouse, jnp.zeros((spare,), jnp.float32)])
    head_cot = jnp.concatenate(
        [
            human_grad.reshape(bin_count, human_tracks),
            mouse_grad.reshape(bin_count, mouse_tracks),
            jnp.zeros((bin_count, spare), jnp.bfloat16),
        ],
        axis=1,
    )
    flat_in = features.astype(jnp.float32).reshape(bin_count, model_width)
    channel_sum, square_sum = place.total(
        jnp.stack([jnp.sum(flat_in, 0), jnp.sum(flat_in * flat_in, 0)])
    )
    channel_mean = channel_sum / token_total
    inv_std = lax.rsqrt(square_sum / token_total - channel_mean * channel_mean + 1e-05)
    batch_hat = (flat_in - channel_mean) * inv_std
    normed = batch_hat * batch_gain + batch_bias
    first_hat, first_scale = norm_parts(normed)
    attn_in = (first_hat * first_gain + first_bias).astype(jnp.bfloat16)

    wide = window_width(length, bin_count)
    distance = (jnp.arange(length + wide) - (length - 1)).astype(jnp.float32)
    basis_low = position_basis(distance, w_position.shape[0], length).astype(jnp.bfloat16)
    position_mine = lax.dynamic_slice_in_dim(w_position, place.seq * kw, kw, 1)
    rel_keys = matmul(basis_low, position_mine).astype(jnp.bfloat16)

    mixed = matmul(attn_in, attn_full)
    group = 2 * kw + vw
    packed = []
    for g in range(seq_count):
        queries = mixed[:, g * group : g * group + kw] * key_scale
        heads_at = slice(g * heads, (g + 1) * heads)
        packed.append(
            jnp.concatenate(
                [
                    (queries + content_bias[heads_at].reshape(kw)).astype(jnp.bfloat16),
                    (queries + position_bias[heads_at].reshape(kw)).astype(jnp.bfloat16),
                    mixed[:, g * group + kw : (g + 1) * group].astype(jnp.bfloat16),
                ],
                axis=1,
            )
        )

    def swap(pieces):
        return [p if m == 0 else place.across(p, m) for m, p in enumerate(pieces)]

    pieces = swap(place.by_seq(packed))
    spot = place.seq.astype(jnp.int32).reshape(1)
    mixed_pieces, probs = attend(pieces, rel_keys, spot, heads, key_size, value_size)
    attended = jnp.concatenate(place.by_seq(swap(mixed_pieces)), axis=1)

    resid = normed + matmul(attended, out_full) + b_out
    second_hat, second_scale = norm_parts(resid)
    mlp_in = (second_hat * second_gain + second_bias).astype(jnp.bfloat16)
    hidden = matmul(mlp_in, up_full) + b_up
    gated = jax.nn.sigmoid(1.702 * hidden)
    middle = (hidden * gated).astype(jnp.bfloat16)
    layer = resid + matmul(middle, down_full) + b_down
    layer_low = layer.astype(jnp.bfloat16)
    positions = place.seq * bin_count + jnp.arange(bin_count)
    inside = (positions >= crop_start[0]) & (positions < crop_start[0] + CROP)
    track = jnp.arange(tracks)
    wanted = jnp.where(track < human_tracks, 0, 1)
    mask = (inside[:, None] & (wanted[None, :] == species[0])).astype(jnp.float32)
    logit = matmul(layer_low, head_full) + head_bias
    head_delta = (mask * head_cot.astype(jnp.float32) * jax.nn.sigmoid(logit)).astype(jnp.bfloat16)
    head_rows = lax.psum_scatter(
        matmul(layer_low.T, head_delta).astype(jnp.bfloat16),
        ("seq", "win"),
        scatter_dimension=0,
        tiled=True,
    ).astype(jnp.float32)
    head_bias_grad = jnp.sum(head_delta.astype(jnp.float32), 0)
    layer_grad = matmul(head_delta, head_full.T)
    down_delta = layer_grad.astype(jnp.bfloat16)
    down_rows = scatter_grad(place, middle, down_delta)
    down_bias_grad = jnp.sum(down_delta.astype(jnp.float32), 0)
    middle_grad = matmul(down_delta, down_full.T)
    hidden_delta = (middle_grad * (gated + 1.702 * hidden * gated * (1.0 - gated))).astype(
        jnp.bfloat16
    )
    up_rows = scatter_grad(place, mlp_in, hidden_delta)
    up_bias_grad = jnp.sum(hidden_delta.astype(jnp.float32), 0)
    mlp_in_grad = matmul(hidden_delta, up_full.T)
    resid_grad, second_gain_grad, second_bias_grad = norm_back(
        layer_grad, mlp_in_grad, second_hat, second_scale, second_gain
    )
    out_delta = resid_grad.astype(jnp.bfloat16)
    out_rows = scatter_grad(place, attended, out_delta)
    out_bias_grad = jnp.sum(out_delta.astype(jnp.float32), 0)
    attended_delta = matmul(out_delta, out_full.T).astype(jnp.bfloat16)
    grads = swap(place.by_seq([attended_delta[:, g * vw : (g + 1) * vw] for g in range(seq_count)]))
    delta_pieces, rel_grad, head_sums = attend_back(
        pieces, grads, rel_keys, probs, spot, heads, key_size, value_size
    )
    attn_delta = jnp.concatenate(place.by_seq(swap(delta_pieces)), axis=1)
    attn_rows = scatter_grad(place, attn_in, attn_delta)
    attn_grad = matmul(attn_delta, attn_full.T)
    normed_grad, first_gain_grad, first_bias_grad = norm_back(
        resid_grad, attn_grad, first_hat, first_scale, first_gain
    )

    early = place.total(
        jnp.concatenate(
            [
                head_bias_grad,
                down_bias_grad,
                up_bias_grad,
                second_gain_grad,
                second_bias_grad,
                out_bias_grad,
            ]
        )
    )
    sizes = [human_tracks, mouse_tracks, spare, model_width, up_bias_grad.shape[0]] + [
        model_width
    ] * 3
    ends = [sum(sizes[: i + 1]) for i in range(len(sizes))]
    (
        human_bias_total,
        mouse_bias_total,
        _,
        down_bias_total,
        up_bias_total,
        second_gain_total,
        second_bias_total,
        out_bias_total,
    ) = [early[end - size : end] for end, size in zip(ends, sizes)]

    position_weight_grad = lax.dot_general(
        rel_grad,
        basis_low.astype(jnp.float32),
        (((1,), (0,)), ((), ())),
        precision=lax.Precision.HIGHEST,
        preferred_element_type=jnp.float32,
    )
    per_head = place.total(
        jnp.concatenate([position_weight_grad, head_sums[:2].T], axis=1), over_seq=False
    )
    per_head = [per_head] + [place.across(per_head, m) for m in range(1, seq_count)]
    per_head = jnp.concatenate(place.by_seq(per_head), axis=0)
    features_count = w_position.shape[0]
    position_total = per_head[:, :features_count].T
    content_total = per_head[:, features_count].reshape(head_count, key_size)
    position_bias_total = per_head[:, features_count + 1].reshape(head_count, key_size)

    late = place.total(
        jnp.stack(
            [
                jnp.sum(normed_grad * batch_hat, 0),
                jnp.sum(normed_grad, 0),
                first_gain_grad,
                first_bias_grad,
            ]
        )
    )
    batch_gain_total, batch_bias_total, first_gain_total, first_bias_total = late
    scaled_grad = normed_grad * batch_gain
    input_grad = inv_std * (
        scaled_grad
        - batch_gain * batch_bias_total / token_total
        - batch_hat * batch_gain * batch_gain_total / token_total
    )
    attn_rows = attn_rows.reshape(shard_rows, seq_count, 2 * kw + vw)
    return (
        layer_low.reshape(windows, bin_count, model_width),
        input_grad.astype(jnp.bfloat16).reshape(windows, bin_count, model_width),
        batch_gain_total,
        batch_bias_total,
        first_gain_total,
        first_bias_total,
        attn_rows[:, :, :kw].reshape(shard_rows, -1),
        attn_rows[:, :, kw : 2 * kw].reshape(shard_rows, -1),
        attn_rows[:, :, 2 * kw :].reshape(shard_rows, -1),
        position_total,
        content_total,
        position_bias_total,
        out_rows,
        out_bias_total,
        second_gain_total,
        second_bias_total,
        up_rows,
        up_bias_total,
        down_rows,
        down_bias_total,
        head_rows[:, :human_tracks],
        human_bias_total,
        head_rows[:, human_tracks : human_tracks + mouse_tracks],
        mouse_bias_total,
    )


def solution(mesh):
    in_specs = (
        P("win", "seq", None),
        P("win"),
        P("win"),
        P("win", "seq", None),
        P("win", "seq", None),
        P(),
        P(),
        P(),
        P(),
        P(("seq", "win"), None),
        P(("seq", "win"), None),
        P(("seq", "win"), None),
        P(),
        P(),
        P(),
        P(("seq", "win"), None),
        P(),
        P(),
        P(),
        P(("seq", "win"), None),
        P(),
        P(("seq", "win"), None),
        P(),
        P(("seq", "win"), None),
        P(),
        P(("seq", "win"), None),
        P(),
    )
    out_specs = (
        P("win", "seq", None),
        P("win", "seq", None),
        P(),
        P(),
        P(),
        P(),
        P(("seq", "win"), None),
        P(("seq", "win"), None),
        P(("seq", "win"), None),
        P(),
        P(),
        P(),
        P(("seq", "win"), None),
        P(),
        P(),
        P(),
        P(("seq", "win"), None),
        P(),
        P(("seq", "win"), None),
        P(),
        P(("seq", "win"), None),
        P(),
        P(("seq", "win"), None),
        P(),
    )
    return jax.shard_map(shards, mesh=mesh, in_specs=in_specs, out_specs=out_specs, check_vma=False)
```

```python
import functools
import math

import jax
import jax.numpy as jnp
from jax import lax
from jax.experimental import pallas as pl
from jax.experimental.pallas import tpu as pltpu
from jax.sharding import PartitionSpec as P

CROP = 896


def position_basis(distance, feature_count, window_length):
    per_kind = feature_count // 6
    magnitude = jnp.abs(distance)[:, None]
    kind_index = jnp.arange(per_kind).astype(jnp.float32)[None, :]
    top_log = math.log2(window_length)
    half_life = 2.0 ** (3.0 + (top_log - 3.0) * kind_index / max(per_kind - 1, 1))
    decays = jnp.exp(-math.log(2.0) * magnitude / half_life)
    widths = 2.0 ** (kind_index + 1.0) - 1.0
    central = jnp.where(widths > magnitude, 1.0, 0.0).astype(jnp.float32)
    centers = window_length * kind_index / per_kind
    spread = window_length / per_kind
    bumps = jnp.exp(-0.5 * ((magnitude - centers) / spread) ** 2)
    even_part = jnp.concatenate([decays, central, bumps], axis=1)
    return jnp.concatenate([even_part, jnp.sign(distance)[:, None] * even_part], axis=1)


def norm_parts(values):
    centered = values - jnp.mean(values, -1, keepdims=True)
    inv_scale = lax.rsqrt(jnp.mean(centered * centered, -1, keepdims=True) + 1e-05)
    return (centered * inv_scale, inv_scale)


def norm_back(outer_grad, inner_grad, normed_hat, inv_scale, gain):
    scaled = inner_grad * gain
    gain_grad = jnp.sum(inner_grad * normed_hat, 0)
    bias_grad = jnp.sum(inner_grad, 0)
    total_grad = outer_grad + inv_scale * (
        scaled
        - jnp.mean(scaled, -1, keepdims=True)
        - normed_hat * jnp.mean(scaled * normed_hat, -1, keepdims=True)
    )
    return (total_grad, gain_grad, bias_grad)


def matmul(left, right):
    return jnp.dot(left, right, preferred_element_type=jnp.float32)


def xor_pairs(count, bit):
    return [(i, i ^ bit) for i in range(count)]


def bits_of(count):
    return [1 << i for i in range(count.bit_length() - 1)]


class Place:
    def __init__(self, shard_rows):
        self.seq_count = lax.axis_size("seq")
        self.win_count = lax.axis_size("win")
        self.seq = lax.axis_index("seq")
        win = lax.axis_index("win")
        self.core = win % 2
        self.ring = self.win_count // 2
        self.chip = win // 2
        self.shard_rows = shard_rows

    def other_core(self, value):
        return lax.ppermute(value, "win", xor_pairs(self.win_count, 1))

    def next_chip(self, value):
        count = self.win_count
        return lax.ppermute(value, "win", [(i, (i + 2) % count) for i in range(count)])

    def last_chip(self, value):
        count = self.win_count
        return lax.ppermute(value, "win", [((i + 2) % count, i) for i in range(count)])

    def same_core(self):
        return [list(range(core, self.win_count, 2)) for core in range(2)]

    def from_chips(self, value):
        return lax.all_gather(value, "win", axis_index_groups=self.same_core())

    def sum_to_chips(self, value):
        return lax.psum_scatter(value, "win", axis_index_groups=self.same_core())

    def across(self, value, bits):
        return lax.ppermute(value, "seq", xor_pairs(self.seq_count, bits))

    def total(self, value, over_seq=True):
        for bit in bits_of(self.win_count):
            value = value + lax.ppermute(value, "win", xor_pairs(self.win_count, bit))
        if over_seq:
            for bit in bits_of(self.seq_count):
                value = value + self.across(value, bit)
        return value

    def by_seq(self, blocks):
        for bit in bits_of(self.seq_count):
            flipped = (self.seq // bit) % 2 == 1
            blocks = [jnp.where(flipped, blocks[m ^ bit], b) for m, b in enumerate(blocks)]
        return blocks


def tie(values, earlier):
    if not earlier:
        return list(values)
    count = len(values)
    anywhere = pl.BlockSpec(memory_space=pl.ANY)
    return pl.pallas_call(
        lambda *refs: None,
        in_specs=[anywhere] * (count + len(earlier)),
        out_specs=[anywhere] * count,
        out_shape=[jax.ShapeDtypeStruct(v.shape, v.dtype) for v in values],
        input_output_aliases={i: i for i in range(count)},
        cost_estimate=pl.CostEstimate(flops=0, bytes_accessed=0, transcendentals=0),
    )(*values, *earlier)


class Steps:
    def __init__(self):
        self.before = []

    def run(self, *jobs):
        values = [v for job in jobs for v in job[0]]
        if not values:
            return
        different = list({id(v): v for v in values}.values())
        held = dict(zip([id(v) for v in different], tie(different, self.before)))
        self.before = []
        for mine, moves, take, *keep in jobs:
            sent = [held[id(v)] for v in mine]
            came = [move(value) for move, value in zip(moves, sent)]
            self.before += came
            if keep:
                keep[0](*sent)
            take(*came)

    def hold(self, *values):
        return tie(values, self.before)


class Gather:
    def __init__(self, place, shard, line=None):
        self.place, self.shard = place, shard
        self.line = [shard] if line is None else line
        self.pieces = []

    def ring_first(self):
        place = self.place
        if place.ring != 4:
            for _ in range(place.ring - 1):
                self.line.append(place.next_chip(self.line[-1]))
            return ((), (), lambda: None)
        return (
            (self.shard, self.shard),
            (place.next_chip, place.last_chip),
            lambda up, down: self.line.extend([up, None, down]),
        )

    def ring_last(self):
        place = self.place
        if place.ring != 4:
            return ((), (), lambda: None)

        def take(value):
            self.line[2] = value

        return ((self.line[1],), (place.next_chip,), take)

    def near(self):
        place, ring = self.place, self.place.ring
        if isinstance(self.line, list):
            line = jnp.stack(self.line[::-1] + self.line[::-1])
            self.line = lax.dynamic_slice_in_dim(line, ring - 1 - place.chip, ring, 0)
        if place.seq_count != 4:
            blocks = [(0, self.line)]
            for bit in bits_of(place.seq_count):
                blocks = blocks + [(m ^ bit, place.across(b, bit)) for m, b in blocks]
            for m, block in blocks:
                self.pieces += [(m, 0, block), (m, 1, place.other_core(block))]
            return ((), (), lambda: None)

        def take(one, two):
            self.one, self.two = one, two

        return (
            (self.line, self.line),
            (lambda v: place.across(v, 1), lambda v: place.across(v, 2)),
            take,
            lambda line, _: setattr(self, "line", line),
        )

    def far(self):
        place = self.place
        if place.seq_count != 4:
            return ((), (), lambda: None)
        half = self.line.shape[-1] // 2

        def take(left, right):
            self.three = jnp.concatenate([left, right], axis=-1)
            self.pieces += [(0, 0, self.line), (1, 0, self.one)]

        return (
            (self.one[..., :half], self.two[..., half:]),
            (lambda v: place.across(v, 2), lambda v: place.across(v, 1)),
            take,
        )

    def core_first(self):
        place = self.place
        if place.seq_count != 4:
            return ((), (), lambda: None)

        def take(both):
            self.pieces += [(0, 1, both[0]), (1, 1, both[1])]

        return ((jnp.stack([self.line, self.one]),), (place.other_core,), take)

    def core_last(self):
        place = self.place
        if place.seq_count != 4:
            return ((), (), lambda: None)

        def take(two, three):
            self.pieces += [(2, 1, two), (3, 1, three)]

        def keep(two, three):
            self.pieces += [(2, 0, two), (3, 0, three)]

        return ((self.two, self.three), (place.other_core, place.other_core), take, keep)

    def whole(self, row, rows, col, width):
        place = self.place
        pieces = [piece for _, _, piece in self.pieces]
        spots = [(m, side) for m, side, _ in self.pieces]
        if rows % 16:
            pieces = [piece[:, row : row + rows] for piece in pieces]
            row = 0
        tile = math.gcd(math.gcd(width, col), 512)
        ring, total = pieces[0].shape[:2]

        def kernel(where_ref, *refs):
            for (m, side), ref in zip(spots, refs):
                refs[-1][where_ref[0] ^ m, :, where_ref[1] ^ side] = ref[:, row : row + rows, :]

        shape = (place.seq_count, ring, 2, rows)
        whole = pl.pallas_call(
            kernel,
            grid_spec=pltpu.PrefetchScalarGridSpec(
                num_scalar_prefetch=1,
                grid=(width // tile,),
                in_specs=[
                    pl.BlockSpec((ring, total, tile), lambda i, *_: (0, 0, i + col // tile))
                    for _ in pieces
                ],
                out_specs=pl.BlockSpec((*shape, tile), lambda i, *_: (0, 0, 0, 0, i)),
            ),
            out_shape=jax.ShapeDtypeStruct((*shape, width), pieces[0].dtype),
            compiler_params=pltpu.CompilerParams(vmem_limit_bytes=VMEM_LIMIT),
            cost_estimate=pl.CostEstimate(
                flops=0, bytes_accessed=4 * math.prod(shape) * width, transcendentals=0
            ),
        )(jnp.stack([place.seq, place.core]).astype(jnp.int32), *pieces)
        return whole.reshape(math.prod(shape), width)


def add_low(*terms):
    return sum(t.astype(jnp.float32) for t in terms).astype(jnp.bfloat16)


class Scatter:
    def __init__(self, place, *pairs):
        self.place = place
        self.pairs = []
        theirs = []
        for inputs, deltas in pairs:
            half = deltas.shape[1] // 2
            low, high = deltas[:, :half], deltas[:, half:]
            self.pairs.append((inputs, jnp.where(place.core == 0, low, high)))
            theirs.append(matmul(inputs.T, jnp.where(place.core == 0, high, low)))
        self.theirs = self.side_by_side(theirs)
        self.half = self.theirs.shape[1]
        rows = place.seq_count * place.win_count * place.shard_rows
        self.rounds = self.theirs.shape[0] // rows
        self.seq_rows = rows // place.seq_count

    def side_by_side(self, parts):
        parts = [p.astype(jnp.bfloat16) for p in parts]
        return parts[0] if len(parts) == 1 else jnp.concatenate(parts, axis=1)

    def cores(self):
        def take(passed):
            sums, at = [], 0
            for inputs, mine in self.pairs:
                size = mine.shape[1]
                sums.append(
                    matmul(inputs.T, mine) + passed[:, at : at + size].astype(jnp.float32)
                )
                at += size
            self.sums = self.side_by_side(sums)
            self.blocks = self.sums.reshape(
                self.rounds, self.place.seq_count, self.seq_rows, self.half
            )

        return ((self.theirs,), (self.place.other_core,), take)

    def block(self, m):
        return lax.dynamic_index_in_dim(self.blocks, self.place.seq ^ m, 1, keepdims=False)

    def far(self):
        place, cut = self.place, self.half // 2
        if place.seq_count != 4:
            return ((), (), lambda: None)
        far = self.block(3)

        def take(by_two, by_one):
            one, two = self.block(1), self.block(2)
            self.one = jnp.concatenate([add_low(one[..., :cut], by_two), one[..., cut:]], axis=-1)
            self.two = jnp.concatenate([two[..., :cut], add_low(two[..., cut:], by_one)], axis=-1)

        return (
            (far[..., :cut], far[..., cut:]),
            (lambda v: place.across(v, 2), lambda v: place.across(v, 1)),
            take,
        )

    def near(self):
        place = self.place
        if place.seq_count != 4:
            blocks = [self.block(m) for m in range(place.seq_count)]
            for bit in bits_of(place.seq_count)[::-1]:
                blocks = [
                    add_low(blocks[m], place.across(blocks[m ^ bit], bit)) for m in range(bit)
                ]
            self.kept = [blocks[0]]
            return ((), (), lambda: None)

        def take(one, two):
            self.kept = [self.block(0), one, two]

        return (
            (self.one, self.two),
            (lambda v: place.across(v, 1), lambda v: place.across(v, 2)),
            take,
        )

    def reduced(self):
        ring = self.place.ring
        total = add_low(*self.kept).reshape(self.rounds, ring, self.seq_rows // ring, self.half)
        return [total[i] for i in range(self.rounds)]


class Stack:
    def __init__(self, place, groups, earlier):
        self.place = place
        blocks = [block for group in groups for block in group.reduced()]
        self.lane = math.gcd(*[b.shape[2] for b in blocks])
        self.counts = [b.shape[2] // self.lane for b in blocks]
        self.rows = [b.shape[1] for b in blocks]
        cut = [
            b[:, :, i * self.lane : (i + 1) * self.lane]
            for b, count in zip(blocks, self.counts)
            for i in range(count)
        ]
        self.total = place.sum_to_chips(tie([jnp.concatenate(cut, axis=1)], earlier)[0])

    def finish(self):
        place, at = self.place, 0
        own, send = [], []
        for rows, count in zip(self.rows, self.counts):
            for _ in range(count):
                upper = self.total[at : at + rows // 2]
                lower = self.total[at + rows // 2 : at + rows]
                at += rows
                own.append(jnp.where(place.core == 0, upper, lower))
                send.append(jnp.where(place.core == 0, lower, upper))

        def take(passed):
            self.results, at, number = [], 0, 0
            for rows, count in zip(self.rows, self.counts):
                mine = jnp.concatenate(own[number : number + count], axis=1)
                number += count
                theirs = []
                for _ in range(count):
                    theirs.append(passed[at : at + rows // 2])
                    at += rows // 2
                theirs = jnp.concatenate(theirs, axis=1)
                first = jnp.where(place.core == 0, mine, theirs)
                second = jnp.where(place.core == 0, theirs, mine)
                self.results.append(
                    jnp.concatenate([first, second], axis=1).astype(jnp.float32)
                )

        return ((jnp.concatenate(send, axis=0),), (place.other_core,), take)


VMEM_LIMIT = 56 * 1024 * 1024


def up_to(value, step):
    return -(-value // step) * step


def dot_last(left, right):
    return lax.dot_general(left, right, (((1,), (1,)), ((), ())), preferred_element_type=jnp.float32)


def dot_plain(left, right):
    return jnp.dot(left, right, preferred_element_type=jnp.float32)


def head_lanes(head, width, total):
    return head * width // 128 * 128, min(up_to((head + 1) * width, 128), total)


def keep_lanes(block, first, low, high):
    lane = lax.broadcasted_iota(jnp.int32, block.shape, 1) + first
    return jnp.where((lane >= low) & (lane < high), block, jnp.zeros_like(block))


def window_width(length, bins):
    return up_to(length + bins + (0 if bins % 128 == 0 else 128), 128)


def window_start(length, bins, here):
    base = length - (here + 1) * bins
    if bins % 128 == 0:
        return pl.multiple_of(base, 128), 0
    start = pl.multiple_of(base // 128 * 128, 128)
    return start, base - start


def attend_kernel(sizes, where_ref, *refs):
    blocks, bins, heads, key_size, value_size, wide = sizes
    length = blocks * bins
    kw, vw = heads * key_size, heads * value_size
    pieces, rel_ref = refs[:blocks], refs[blocks]
    outs, probs_ref, keys, values = refs[blocks + 1 : 2 * blocks + 1], *refs[2 * blocks + 1 :]
    step = pl.program_id(0)
    place = where_ref[0]

    @pl.when(step == 0)
    def _():
        for m in range(blocks):
            rows = pl.ds(pl.multiple_of((place ^ m) * bins, bins), bins)
            keys[rows, :] = pieces[m][:, 2 * kw : 3 * kw]
            values[rows, :] = pieces[m][:, 3 * kw :]

    def one(m):
        here = place ^ m
        base, moved = window_start(length, bins, here)
        window = rel_ref[pl.ds(base, wide), :]
        for head in range(heads):
            low, high = head * key_size, (head + 1) * key_size
            q_content = keep_lanes(pieces[m][:, :kw], 0, low, high)
            q_position = keep_lanes(pieces[m][:, kw : 2 * kw], 0, low, high)
            relative = dot_last(q_position, window)
            relative = pltpu.roll(relative, wide - (bins - 1), 1, stride=1, stride_axis=0)
            if bins % 128:
                relative = pltpu.roll(relative, wide - moved, 1)
            scores = dot_last(q_content, keys[...]) + relative[:, :length]
            top = jnp.max(scores, -1, keepdims=True)
            expo = jnp.exp(scores - top)
            probs = (expo * (1.0 / jnp.sum(expo, -1, keepdims=True))).astype(jnp.bfloat16)
            probs_ref[0, head] = probs
            first, last = head_lanes(head, value_size, vw)
            mixed = dot_plain(probs, values[:, first:last])
            mixed = keep_lanes(mixed, first, head * value_size, (head + 1) * value_size)
            if head == 0:
                outs[m][...] = jnp.zeros_like(outs[m])
            outs[m][:, first:last] += mixed.astype(jnp.bfloat16)

    for m in range(blocks):
        pl.when(step == m)(functools.partial(one, m))


def attend(pieces, rel_keys, place, heads, key_size, value_size):
    blocks, bins = len(pieces), pieces[0].shape[0]
    length = blocks * bins
    wide = window_width(length, bins)
    kw, vw = heads * key_size, heads * value_size
    whole = lambda shape: pl.BlockSpec(shape, lambda i, *_: (0,) * len(shape))
    sizes = (blocks, bins, heads, key_size, value_size, wide)
    flops = 2 * heads * length * length * (2 * key_size + value_size)
    result = pl.pallas_call(
        functools.partial(attend_kernel, sizes),
        grid_spec=pltpu.PrefetchScalarGridSpec(
            num_scalar_prefetch=1,
            grid=(blocks,),
            in_specs=[whole(p.shape) for p in pieces] + [whole(rel_keys.shape)],
            out_specs=[whole((bins, vw))] * blocks
            + [pl.BlockSpec((1, heads, bins, length), lambda i, *_: (i, 0, 0, 0))],
            scratch_shapes=[
                pltpu.VMEM((length, kw), jnp.bfloat16),
                pltpu.VMEM((length, vw), jnp.bfloat16),
            ],
        ),
        out_shape=[jax.ShapeDtypeStruct((bins, vw), jnp.bfloat16)] * blocks
        + [jax.ShapeDtypeStruct((blocks, heads, bins, length), jnp.bfloat16)],
        compiler_params=pltpu.CompilerParams(vmem_limit_bytes=VMEM_LIMIT),
        cost_estimate=pl.CostEstimate(
            flops=flops * 2, bytes_accessed=2 * heads * length * length, transcendentals=heads * length * length
        ),
    )(place, *pieces, rel_keys)
    return result[:blocks], result[blocks]


def attend_back_kernel(sizes, where_ref, *refs):
    blocks, bins, heads, key_size, value_size, wide = sizes
    length = blocks * bins
    kw, vw = heads * key_size, heads * value_size
    key_scale = key_size ** (-0.5)
    pieces, grads, rel_ref, probs_ref = (
        refs[:blocks], refs[blocks : 2 * blocks], refs[2 * blocks], refs[2 * blocks + 1],
    )
    rest = refs[2 * blocks + 2 :]
    outs, rel_grad, sums, keys, values, key_grad, value_grad = rest[:blocks], *rest[blocks:]
    step = pl.program_id(0)
    place = where_ref[0]

    @pl.when(step == 0)
    def _():
        for m in range(blocks):
            rows = pl.ds(pl.multiple_of((place ^ m) * bins, bins), bins)
            keys[rows, :] = pieces[m][:, 2 * kw : 3 * kw]
            values[rows, :] = pieces[m][:, 3 * kw :]
        rel_grad[...] = jnp.zeros_like(rel_grad)
        sums[...] = jnp.zeros_like(sums)
        key_grad[...] = jnp.zeros_like(key_grad)
        value_grad[...] = jnp.zeros_like(value_grad)

    def one(m):
        here = place ^ m
        base, moved = window_start(length, bins, here)
        window = rel_ref[pl.ds(base, wide), :]
        total = None
        row = lax.broadcasted_iota(jnp.int32, (bins, bins), 0)
        col = lax.broadcasted_iota(jnp.int32, (bins, bins), 1)
        flip = jnp.where(row + col == bins - 1, 1.0, 0.0).astype(jnp.bfloat16)
        for head in range(heads):
            low, high = head * key_size, (head + 1) * key_size
            vlow, vhigh = head * value_size, (head + 1) * value_size
            first, last = head_lanes(head, value_size, vw)
            probs = probs_ref[0, head]
            out_grad = keep_lanes(grads[m][:, first:last], first, vlow, vhigh)
            prob_grad = dot_last(out_grad, values[:, first:last])
            probs_f = probs.astype(jnp.float32)
            row_delta = jnp.sum(probs_f * prob_grad, -1, keepdims=True)
            delta = (probs_f * (prob_grad - row_delta)).astype(jnp.bfloat16)
            value_grad[first:last, :] += dot_plain(out_grad.T, probs)
            q_content = keep_lanes(pieces[m][:, :kw], 0, low, high)
            q_position = keep_lanes(pieces[m][:, kw : 2 * kw], 0, low, high)
            key_grad[...] += dot_plain(q_content.T, delta)
            content = keep_lanes(dot_plain(delta, keys[...]), 0, low, high)
            shifted = jnp.concatenate(
                [dot_plain(flip, delta), jnp.zeros((bins, wide - length), jnp.float32)], axis=1
            )
            shifted = pltpu.roll(shifted, 0, 1, stride=1, stride_axis=0)
            if bins % 128:
                shifted = pltpu.roll(shifted, moved, 1)
            shifted = shifted.astype(jnp.bfloat16)
            position = keep_lanes(dot_plain(shifted, window), 0, low, high)
            position = jnp.dot(
                flip.astype(jnp.float32),
                position,
                precision=lax.Precision.HIGHEST,
                preferred_element_type=jnp.float32,
            )
            q_position = dot_plain(flip, q_position).astype(jnp.bfloat16)
            rel_grad[:, pl.ds(base, wide)] += dot_plain(q_position.T, shifted)
            sums[0:1, :] += jnp.sum(content, 0, keepdims=True)
            sums[1:2, :] += jnp.sum(position, 0, keepdims=True)
            both = content + position
            total = both if total is None else total + both
        outs[m][:, :kw] = (total * key_scale).astype(jnp.bfloat16)

    for m in range(blocks):
        pl.when(step == m)(functools.partial(one, m))

    @pl.when(step == blocks - 1)
    def _():
        keys[...] = key_grad[...].T.astype(jnp.bfloat16)
        values[...] = value_grad[...].T.astype(jnp.bfloat16)
        for m in range(blocks):
            rows = pl.ds(pl.multiple_of((place ^ m) * bins, bins), bins)
            outs[m][:, kw : 2 * kw] = keys[rows, :]
            outs[m][:, 2 * kw :] = values[rows, :]


def attend_back(pieces, grads, rel_keys, probs, place, heads, key_size, value_size):
    blocks, bins = len(pieces), pieces[0].shape[0]
    length = blocks * bins
    wide = window_width(length, bins)
    kw, vw = heads * key_size, heads * value_size
    whole = lambda shape: pl.BlockSpec(shape, lambda i, *_: (0,) * len(shape))
    sizes = (blocks, bins, heads, key_size, value_size, wide)
    rel_shape = (kw, rel_keys.shape[0])
    flops = 2 * heads * length * length * (4 * key_size + 2 * value_size)
    result = pl.pallas_call(
        functools.partial(attend_back_kernel, sizes),
        grid_spec=pltpu.PrefetchScalarGridSpec(
            num_scalar_prefetch=1,
            grid=(blocks,),
            in_specs=[whole(p.shape) for p in pieces]
            + [whole(g.shape) for g in grads]
            + [whole(rel_keys.shape)]
            + [pl.BlockSpec((1, heads, bins, length), lambda i, *_: (i, 0, 0, 0))],
            out_specs=[whole((bins, 2 * kw + vw))] * blocks + [whole(rel_shape), whole((8, kw))],
            scratch_shapes=[
                pltpu.VMEM((length, kw), jnp.bfloat16),
                pltpu.VMEM((length, vw), jnp.bfloat16),
                pltpu.VMEM((kw, length), jnp.float32),
                pltpu.VMEM((vw, length), jnp.float32),
            ],
        ),
        out_shape=[jax.ShapeDtypeStruct((bins, 2 * kw + vw), jnp.bfloat16)] * blocks
        + [jax.ShapeDtypeStruct(rel_shape, jnp.float32), jax.ShapeDtypeStruct((8, kw), jnp.float32)],
        compiler_params=pltpu.CompilerParams(vmem_limit_bytes=VMEM_LIMIT),
        cost_estimate=pl.CostEstimate(
            flops=flops * 2, bytes_accessed=2 * heads * length * length, transcendentals=0
        ),
    )(place, *pieces, *grads, rel_keys, probs)
    return result[:blocks], result[blocks], result[blocks + 1]


def heads_kernel(sizes, where_ref, layer, weight, bias, human, mouse, out_grad, grad, bias_grad, turned):
    tile, human_tiles, human_tracks, mouse_tracks = sizes
    step = pl.program_id(0)
    species, first, last = where_ref[0], where_ref[1], where_ref[2]
    is_human = step < human_tiles

    @pl.when(step == 0)
    def _():
        turned[...] = layer[...].T
        grad[...] = jnp.zeros_like(grad)

    wanted = jnp.where(is_human, 0, 1) == species

    def one(cotangent, start, tracks):
        logit = dot_plain(layer[...], weight[...]) + bias[...]
        row = lax.broadcasted_iota(jnp.int32, logit.shape, 0)
        col = lax.broadcasted_iota(jnp.int32, logit.shape, 1) + start
        inside = (row >= first) & (row < last) & (col < tracks)
        scale = cotangent[...].astype(jnp.float32) * (1.0 / (1.0 + jnp.exp(-logit)))
        delta_f = jnp.where(inside, scale, 0.0)
        delta = delta_f.astype(jnp.bfloat16)
        bias_grad[...] = jnp.sum(delta.astype(jnp.float32), 0, keepdims=True)
        out_grad[...] = dot_plain(turned[...], delta).astype(jnp.bfloat16)
        grad[...] += dot_last(delta, weight[...])

    @pl.when(wanted & is_human)
    def _():
        one(human, step * tile, human_tracks)

    @pl.when(wanted & jnp.logical_not(is_human))
    def _():
        one(mouse, (step - human_tiles) * tile, mouse_tracks)

    @pl.when(jnp.logical_not(wanted))
    def _():
        out_grad[...] = jnp.zeros_like(out_grad)
        bias_grad[...] = jnp.zeros_like(bias_grad)


def both_heads(layer, weight, bias, human, mouse, where, tile):
    rows, width = layer.shape
    human_tiles = -(-human.shape[1] // tile)
    mouse_tiles = -(-mouse.shape[1] // tile)
    tiles = human_tiles + mouse_tiles
    sizes = (tile, human_tiles, human.shape[1], mouse.shape[1])
    return pl.pallas_call(
        functools.partial(heads_kernel, sizes),
        grid_spec=pltpu.PrefetchScalarGridSpec(
            num_scalar_prefetch=1,
            grid=(tiles,),
            in_specs=[
                pl.BlockSpec((rows, width), lambda i, *_: (0, 0)),
                pl.BlockSpec((width, tile), lambda i, *_: (0, i)),
                pl.BlockSpec((1, tile), lambda i, *_: (0, i)),
                pl.BlockSpec((rows, tile), lambda i, *_: (0, jnp.minimum(i, human_tiles - 1))),
                pl.BlockSpec((rows, tile), lambda i, *_: (0, jnp.maximum(i - human_tiles, 0))),
            ],
            out_specs=[
                pl.BlockSpec((width, tile), lambda i, *_: (0, i)),
                pl.BlockSpec((rows, width), lambda i, *_: (0, 0)),
                pl.BlockSpec((1, tile), lambda i, *_: (0, i)),
            ],
            scratch_shapes=[pltpu.VMEM((width, rows), jnp.bfloat16)],
        ),
        out_shape=[
            jax.ShapeDtypeStruct((width, tiles * tile), jnp.bfloat16),
            jax.ShapeDtypeStruct((rows, width), jnp.float32),
            jax.ShapeDtypeStruct((1, tiles * tile), jnp.float32),
        ],
        compiler_params=pltpu.CompilerParams(vmem_limit_bytes=VMEM_LIMIT),
        cost_estimate=pl.CostEstimate(
            flops=6 * rows * width * tiles * tile,
            bytes_accessed=4 * width * tiles * tile,
            transcendentals=rows * tiles * tile,
        ),
    )(where, layer, weight, bias, human, mouse)


def shards(
    features,
    species,
    crop_start,
    human_grad,
    mouse_grad,
    batch_gain,
    batch_bias,
    first_gain,
    first_bias,
    w_query,
    w_key,
    w_value,
    w_position,
    content_bias,
    position_bias,
    w_out,
    b_out,
    second_gain,
    second_bias,
    w_up,
    b_up,
    w_down,
    b_down,
    w_human,
    b_human,
    w_mouse,
    b_mouse,
):
    place = Place(w_query.shape[0])
    seq_count = place.seq_count
    windows, bin_count, model_width = features.shape
    assert windows == 1
    head_count, key_size = content_bias.shape
    value_size = model_width // head_count
    length = bin_count * seq_count
    token_total = bin_count * seq_count * place.win_count
    key_scale = key_size ** (-0.5)
    heads = head_count // seq_count
    kw, vw = heads * key_size, heads * value_size
    human_tracks, mouse_tracks = b_human.shape[0], b_mouse.shape[0]
    tile = 896
    human_wide, mouse_wide = up_to(human_tracks, tile), up_to(mouse_tracks, tile)
    tracks = human_wide + mouse_wide

    def side_by_side(human, mouse):
        return jnp.concatenate(
            [
                jnp.pad(human, [(0, 0)] * (human.ndim - 1) + [(0, human_wide - human_tracks)]),
                jnp.pad(mouse, [(0, 0)] * (mouse.ndim - 1) + [(0, mouse_wide - mouse_tracks)]),
            ],
            axis=-1,
        )

    shard_rows = w_query.shape[0]
    attn_shard = jnp.concatenate(
        [
            w_query.reshape(shard_rows, seq_count, kw),
            w_key.reshape(shard_rows, seq_count, kw),
            w_value.reshape(shard_rows, seq_count, vw),
        ],
        axis=2,
    ).reshape(shard_rows, -1)
    head_shard = side_by_side(w_human, w_mouse)
    attn_width, up_width = attn_shard.shape[1], w_up.shape[1]
    devices = seq_count * place.win_count
    rounds = w_down.shape[0] // shard_rows

    def to_rounds(value):
        split = value.reshape(*value.shape[:-1], devices, rounds, shard_rows)
        return jnp.swapaxes(split, -3, -2).reshape(value.shape)

    def from_rounds(value):
        split = value.reshape(*value.shape[:-1], rounds, devices, shard_rows)
        return jnp.swapaxes(split, -3, -2).reshape(value.shape)

    down_parts = [w_down[i * shard_rows : (i + 1) * shard_rows] for i in range(rounds)]
    late_shard = jnp.concatenate([head_shard, to_rounds(w_up), *down_parts], axis=1)
    late_full = lax.all_gather(late_shard, ("seq", "win"), axis=0, tiled=True)
    up_full = late_full[:, tracks : tracks + up_width]
    down_at = tracks + up_width
    down_full = [
        late_full[:, down_at + i * model_width : down_at + (i + 1) * model_width]
        for i in range(rounds)
    ]
    steps = Steps()
    first_w = Gather(place, jnp.concatenate([attn_shard, w_out], axis=1))
    steps.run(first_w.ring_first())
    steps.run(first_w.ring_last())
    flat_in = features.astype(jnp.float32).reshape(bin_count, model_width)
    channel_sum, square_sum = place.total(
        jnp.stack([jnp.sum(flat_in, 0), jnp.sum(flat_in * flat_in, 0)])
    )
    channel_mean = channel_sum / token_total
    inv_std = lax.rsqrt(square_sum / token_total - channel_mean * channel_mean + 1e-05)
    batch_hat = (flat_in - channel_mean) * inv_std
    normed = batch_hat * batch_gain + batch_bias
    first_hat, first_scale = norm_parts(normed)
    attn_in = (first_hat * first_gain + first_bias).astype(jnp.bfloat16)

    wide = window_width(length, bin_count)
    distance = (jnp.arange(length + wide) - (length - 1)).astype(jnp.float32)
    basis_low = position_basis(distance, w_position.shape[0], length).astype(jnp.bfloat16)
    position_mine = lax.dynamic_slice_in_dim(w_position, place.seq * kw, kw, 1)
    rel_keys = matmul(basis_low, position_mine).astype(jnp.bfloat16)

    steps.run(first_w.near())
    steps.before.append(attn_in)
    steps.run(first_w.far(), first_w.core_first())
    steps.run(first_w.core_last())
    attn_full = first_w.whole(0, shard_rows, 0, attn_width)
    out_full = first_w.whole(0, shard_rows, attn_width, model_width)
    mixed = matmul(attn_in, attn_full)
    group = 2 * kw + vw
    packed = []
    for g in range(seq_count):
        queries = mixed[:, g * group : g * group + kw] * key_scale
        heads_at = slice(g * heads, (g + 1) * heads)
        packed.append(
            jnp.concatenate(
                [
                    (queries + content_bias[heads_at].reshape(kw)).astype(jnp.bfloat16),
                    (queries + position_bias[heads_at].reshape(kw)).astype(jnp.bfloat16),
                    mixed[:, g * group + kw : (g + 1) * group].astype(jnp.bfloat16),
                ],
                axis=1,
            )
        )

    def swap(pieces):
        results = list(pieces[:1])
        moves = [functools.partial(place.across, bits=m) for m in range(1, seq_count)]
        return (pieces[1:], moves, lambda *came: results.extend(came)), results

    job, pieces = swap(place.by_seq(packed))
    steps.run(job)
    spot = place.seq.astype(jnp.int32).reshape(1)
    mixed_pieces, probs = attend(pieces, rel_keys, spot, heads, key_size, value_size)
    job, mixed_pieces = swap(mixed_pieces)
    steps.run(job)
    attended = jnp.concatenate(place.by_seq(mixed_pieces), axis=1)
    resid = normed + matmul(attended, out_full) + b_out
    second_hat, second_scale = norm_parts(resid)
    mlp_in = (second_hat * second_gain + second_bias).astype(jnp.bfloat16)
    hidden = matmul(mlp_in, up_full) + to_rounds(b_up)
    gated = jax.nn.sigmoid(1.702 * hidden)
    middle = (hidden * gated).astype(jnp.bfloat16)
    layer = resid + b_down
    for i, part in enumerate(down_full):
        layer = layer + matmul(middle[:, i * model_width : (i + 1) * model_width], part)
    layer_low = layer.astype(jnp.bfloat16)
    first_row = crop_start[0] - place.seq * bin_count
    head_grad, layer_grad, head_bias_grad = both_heads(
        layer_low,
        late_full,
        side_by_side(b_human, b_mouse)[None],
        human_grad.reshape(bin_count, human_tracks),
        mouse_grad.reshape(bin_count, mouse_tracks),
        jnp.stack([species[0], first_row, first_row + CROP]).astype(jnp.int32),
        tile,
    )
    head_bias_grad = head_bias_grad[0]
    head_rows = lax.psum_scatter(head_grad, ("seq", "win"), scatter_dimension=0, tiled=True)
    down_delta = layer_grad.astype(jnp.bfloat16)
    down = Scatter(place, (middle, down_delta))
    steps.run(down.cores())
    down_bias_grad = jnp.sum(down_delta.astype(jnp.float32), 0)
    middle_grad = jnp.concatenate([matmul(down_delta, part.T) for part in down_full], axis=1)
    hidden_delta = (middle_grad * (gated + 1.702 * hidden * gated * (1.0 - gated))).astype(
        jnp.bfloat16
    )
    up = Scatter(place, (mlp_in, hidden_delta))
    steps.run(down.far(), up.cores())
    up_bias_grad = jnp.sum(hidden_delta.astype(jnp.float32), 0)
    mlp_in_grad = matmul(hidden_delta, up_full.T)
    resid_grad, second_gain_grad, second_bias_grad = norm_back(
        layer_grad, mlp_in_grad, second_hat, second_scale, second_gain
    )
    out_delta = resid_grad.astype(jnp.bfloat16)
    out = Scatter(place, (attended, out_delta))
    out_bias_grad = jnp.sum(out_delta.astype(jnp.float32), 0)
    attended_delta = matmul(out_delta, out_full.T).astype(jnp.bfloat16)
    job, grads = swap(
        place.by_seq([attended_delta[:, g * vw : (g + 1) * vw] for g in range(seq_count)])
    )
    steps.run(job)
    steps.run(down.near(), up.far(), out.cores())
    delta_pieces, rel_grad, head_sums = attend_back(
        pieces, grads, rel_keys, probs, spot, heads, key_size, value_size
    )
    *delta_pieces, rel_grad, head_sums = steps.hold(*delta_pieces, rel_grad, head_sums)
    job, delta_pieces = swap(delta_pieces)
    steps.run(job, up.near())
    first_stack = Stack(place, (down, up), [head_rows])
    attn_delta = jnp.concatenate(place.by_seq(delta_pieces), axis=1)
    attn = Scatter(place, (attn_in, attn_delta))
    steps.run(out.far(), attn.cores())
    steps.run(out.near(), attn.far())
    steps.run(attn.near())
    second_stack = Stack(place, (out, attn), [first_stack.total])
    steps.run(first_stack.finish())
    steps.run(second_stack.finish())
    *down_rows, up_rows = first_stack.results
    down_rows = jnp.concatenate(down_rows, axis=0)
    up_rows = from_rounds(up_rows)
    out_rows, attn_rows = second_stack.results
    head_rows = head_rows.astype(jnp.float32)
    attn_grad = matmul(attn_delta, attn_full.T)
    normed_grad, first_gain_grad, first_bias_grad = norm_back(
        resid_grad, attn_grad, first_hat, first_scale, first_gain
    )

    position_weight_grad = lax.dot_general(
        rel_grad,
        basis_low.astype(jnp.float32),
        (((1,), (0,)), ((), ())),
        precision=lax.Precision.HIGHEST,
        preferred_element_type=jnp.float32,
    )
    per_head = place.total(
        jnp.concatenate([position_weight_grad, head_sums[:2].T], axis=1), over_seq=False
    )
    per_head = [per_head] + [place.across(per_head, m) for m in range(1, seq_count)]
    per_head = jnp.concatenate(place.by_seq(per_head), axis=0)
    features_count = w_position.shape[0]
    position_total = per_head[:, :features_count].T
    content_total = per_head[:, features_count].reshape(head_count, key_size)
    position_bias_total = per_head[:, features_count + 1].reshape(head_count, key_size)

    parts = [
        jnp.sum(normed_grad * batch_hat, 0),
        jnp.sum(normed_grad, 0),
        first_gain_grad,
        first_bias_grad,
        head_bias_grad[:human_tracks],
        head_bias_grad[human_wide : human_wide + mouse_tracks],
        down_bias_grad,
        up_bias_grad,
        second_gain_grad,
        second_bias_grad,
        out_bias_grad,
    ]
    ends = [0]
    for part in parts:
        ends.append(ends[-1] + up_to(part.shape[0], 1024))
    totals = place.total(
        jnp.concatenate([jnp.pad(p, (0, up_to(p.shape[0], 1024) - p.shape[0])) for p in parts])
    )
    (
        batch_gain_total,
        batch_bias_total,
        first_gain_total,
        first_bias_total,
        human_bias_total,
        mouse_bias_total,
        down_bias_total,
        up_bias_total,
        second_gain_total,
        second_bias_total,
        out_bias_total,
    ) = [totals[at : at + p.shape[0]] for at, p in zip(ends, parts)]
    scaled_grad = normed_grad * batch_gain
    input_grad = inv_std * (
        scaled_grad
        - batch_gain * batch_bias_total / token_total
        - batch_hat * batch_gain * batch_gain_total / token_total
    )
    attn_rows = attn_rows.reshape(shard_rows, seq_count, 2 * kw + vw)
    return (
        layer_low.reshape(windows, bin_count, model_width),
        input_grad.astype(jnp.bfloat16).reshape(windows, bin_count, model_width),
        batch_gain_total,
        batch_bias_total,
        first_gain_total,
        first_bias_total,
        attn_rows[:, :, :kw].reshape(shard_rows, -1),
        attn_rows[:, :, kw : 2 * kw].reshape(shard_rows, -1),
        attn_rows[:, :, 2 * kw :].reshape(shard_rows, -1),
        position_total,
        content_total,
        position_bias_total,
        out_rows,
        out_bias_total,
        second_gain_total,
        second_bias_total,
        up_rows,
        from_rounds(up_bias_total),
        down_rows,
        down_bias_total,
        head_rows[:, :human_tracks],
        human_bias_total,
        head_rows[:, human_wide : human_wide + mouse_tracks],
        mouse_bias_total,
    )


def solution(mesh):
    in_specs = (
        P("win", "seq", None),
        P("win"),
        P("win"),
        P("win", "seq", None),
        P("win", "seq", None),
        P(),
        P(),
        P(),
        P(),
        P(("seq", "win"), None),
        P(("seq", "win"), None),
        P(("seq", "win"), None),
        P(),
        P(),
        P(),
        P(("seq", "win"), None),
        P(),
        P(),
        P(),
        P(("seq", "win"), None),
        P(),
        P(("seq", "win"), None),
        P(),
        P(("seq", "win"), None),
        P(),
        P(("seq", "win"), None),
        P(),
    )
    out_specs = (
        P("win", "seq", None),
        P("win", "seq", None),
        P(),
        P(),
        P(),
        P(),
        P(("seq", "win"), None),
        P(("seq", "win"), None),
        P(("seq", "win"), None),
        P(),
        P(),
        P(),
        P(("seq", "win"), None),
        P(),
        P(),
        P(),
        P(("seq", "win"), None),
        P(),
        P(("seq", "win"), None),
        P(),
        P(("seq", "win"), None),
        P(),
        P(("seq", "win"), None),
        P(),
    )
    return jax.shard_map(shards, mesh=mesh, in_specs=in_specs, out_specs=out_specs, check_vma=False)
```

```python
import functools
import math

import jax
import jax.numpy as jnp
from jax import lax
from jax.experimental import pallas as pl
from jax.experimental.pallas import tpu as pltpu
from jax.sharding import PartitionSpec as P

CROP = 896


def position_basis(distance, feature_count, window_length):
    per_kind = feature_count // 6
    magnitude = jnp.abs(distance)[:, None]
    kind_index = jnp.arange(per_kind).astype(jnp.float32)[None, :]
    top_log = math.log2(window_length)
    half_life = 2.0 ** (3.0 + (top_log - 3.0) * kind_index / max(per_kind - 1, 1))
    decays = jnp.exp(-math.log(2.0) * magnitude / half_life)
    widths = 2.0 ** (kind_index + 1.0) - 1.0
    central = jnp.where(widths > magnitude, 1.0, 0.0).astype(jnp.float32)
    centers = window_length * kind_index / per_kind
    spread = window_length / per_kind
    bumps = jnp.exp(-0.5 * ((magnitude - centers) / spread) ** 2)
    even_part = jnp.concatenate([decays, central, bumps], axis=1)
    return jnp.concatenate([even_part, jnp.sign(distance)[:, None] * even_part], axis=1)


def norm_parts(values):
    centered = values - jnp.mean(values, -1, keepdims=True)
    inv_scale = lax.rsqrt(jnp.mean(centered * centered, -1, keepdims=True) + 1e-05)
    return (centered * inv_scale, inv_scale)


def norm_back(outer_grad, inner_grad, normed_hat, inv_scale, gain):
    scaled = inner_grad * gain
    gain_grad = jnp.sum(inner_grad * normed_hat, 0)
    bias_grad = jnp.sum(inner_grad, 0)
    total_grad = outer_grad + inv_scale * (
        scaled
        - jnp.mean(scaled, -1, keepdims=True)
        - normed_hat * jnp.mean(scaled * normed_hat, -1, keepdims=True)
    )
    return (total_grad, gain_grad, bias_grad)


def matmul(left, right):
    return jnp.dot(left, right, preferred_element_type=jnp.float32)


def xor_pairs(count, bit):
    return [(i, i ^ bit) for i in range(count)]


def bits_of(count):
    return [1 << i for i in range(count.bit_length() - 1)]


class Place:
    def __init__(self, shard_rows):
        self.seq_count = lax.axis_size("seq")
        self.win_count = lax.axis_size("win")
        self.seq = lax.axis_index("seq")
        win = lax.axis_index("win")
        self.core = win % 2
        self.ring = self.win_count // 2
        self.chip = win // 2
        self.shard_rows = shard_rows

    def other_core(self, value):
        return lax.ppermute(value, "win", xor_pairs(self.win_count, 1))

    def next_chip(self, value):
        count = self.win_count
        return lax.ppermute(value, "win", [(i, (i + 2) % count) for i in range(count)])

    def last_chip(self, value):
        count = self.win_count
        return lax.ppermute(value, "win", [((i + 2) % count, i) for i in range(count)])

    def same_core(self):
        return [list(range(core, self.win_count, 2)) for core in range(2)]

    def from_chips(self, value):
        return lax.all_gather(value, "win", axis_index_groups=self.same_core())

    def sum_to_chips(self, value):
        return lax.psum_scatter(value, "win", axis_index_groups=self.same_core())

    def across(self, value, bits):
        return lax.ppermute(value, "seq", xor_pairs(self.seq_count, bits))

    def total(self, value, over_seq=True):
        for bit in bits_of(self.win_count):
            value = value + lax.ppermute(value, "win", xor_pairs(self.win_count, bit))
        if over_seq:
            for bit in bits_of(self.seq_count):
                value = value + self.across(value, bit)
        return value

    def by_seq(self, blocks):
        for bit in bits_of(self.seq_count):
            flipped = (self.seq // bit) % 2 == 1
            blocks = [jnp.where(flipped, blocks[m ^ bit], b) for m, b in enumerate(blocks)]
        return blocks


def tie(values, earlier):
    if not earlier:
        return list(values)
    count = len(values)
    anywhere = pl.BlockSpec(memory_space=pl.ANY)
    return pl.pallas_call(
        lambda *refs: None,
        in_specs=[anywhere] * (count + len(earlier)),
        out_specs=[anywhere] * count,
        out_shape=[jax.ShapeDtypeStruct(v.shape, v.dtype) for v in values],
        input_output_aliases={i: i for i in range(count)},
        cost_estimate=pl.CostEstimate(flops=0, bytes_accessed=0, transcendentals=0),
    )(*values, *earlier)


class Steps:
    def __init__(self):
        self.before = []

    def run(self, *jobs):
        values = [v for job in jobs for v in job[0]]
        if not values:
            return
        different = list({id(v): v for v in values}.values())
        held = dict(zip([id(v) for v in different], tie(different, self.before)))
        self.before = []
        for mine, moves, take, *keep in jobs:
            sent = [held[id(v)] for v in mine]
            came = [move(value) for move, value in zip(moves, sent)]
            self.before += came
            if keep:
                keep[0](*sent)
            take(*came)

    def hold(self, *values):
        return tie(values, self.before)


class Gather:
    def __init__(self, place, shard, line=None):
        self.place, self.shard = place, shard
        self.line = [shard] if line is None else line
        self.pieces = []

    def ring_first(self):
        place = self.place
        if place.ring != 4:
            for _ in range(place.ring - 1):
                self.line.append(place.next_chip(self.line[-1]))
            return ((), (), lambda: None)
        return (
            (self.shard, self.shard),
            (place.next_chip, place.last_chip),
            lambda up, down: self.line.extend([up, None, down]),
        )

    def ring_last(self):
        place = self.place
        if place.ring != 4:
            return ((), (), lambda: None)

        def take(value):
            self.line[2] = value

        return ((self.line[1],), (place.next_chip,), take)

    def near(self):
        place, ring = self.place, self.place.ring
        if isinstance(self.line, list):
            line = jnp.stack(self.line[::-1] + self.line[::-1])
            self.line = lax.dynamic_slice_in_dim(line, ring - 1 - place.chip, ring, 0)
        if place.seq_count != 4:
            blocks = [(0, self.line)]
            for bit in bits_of(place.seq_count):
                blocks = blocks + [(m ^ bit, place.across(b, bit)) for m, b in blocks]
            for m, block in blocks:
                self.pieces += [(m, 0, block), (m, 1, place.other_core(block))]
            return ((), (), lambda: None)

        def take(one, two):
            self.one, self.two = one, two

        return (
            (self.line, self.line),
            (lambda v: place.across(v, 1), lambda v: place.across(v, 2)),
            take,
            lambda line, _: setattr(self, "line", line),
        )

    def far(self):
        place = self.place
        if place.seq_count != 4:
            return ((), (), lambda: None)
        half = self.line.shape[-1] // 2

        def take(left, right):
            self.three = jnp.concatenate([left, right], axis=-1)
            self.pieces += [(0, 0, self.line), (1, 0, self.one)]

        return (
            (self.one[..., :half], self.two[..., half:]),
            (lambda v: place.across(v, 2), lambda v: place.across(v, 1)),
            take,
        )

    def core_first(self):
        place = self.place
        if place.seq_count != 4:
            return ((), (), lambda: None)

        def take(both):
            self.pieces += [(0, 1, both[0]), (1, 1, both[1])]

        return ((jnp.stack([self.line, self.one]),), (place.other_core,), take)

    def core_last(self):
        place = self.place
        if place.seq_count != 4:
            return ((), (), lambda: None)

        def take(two, three):
            self.pieces += [(2, 1, two), (3, 1, three)]

        def keep(two, three):
            self.pieces += [(2, 0, two), (3, 0, three)]

        return ((self.two, self.three), (place.other_core, place.other_core), take, keep)

    def whole(self, row, rows, col, width):
        place = self.place
        pieces = [piece for _, _, piece in self.pieces]
        spots = [(m, side) for m, side, _ in self.pieces]
        if rows % 16:
            pieces = [piece[:, row : row + rows] for piece in pieces]
            row = 0
        tile = math.gcd(math.gcd(width, col), 512)
        ring, total = pieces[0].shape[:2]

        def kernel(where_ref, *refs):
            for (m, side), ref in zip(spots, refs):
                refs[-1][where_ref[0] ^ m, :, where_ref[1] ^ side] = ref[:, row : row + rows, :]

        shape = (place.seq_count, ring, 2, rows)
        whole = pl.pallas_call(
            kernel,
            grid_spec=pltpu.PrefetchScalarGridSpec(
                num_scalar_prefetch=1,
                grid=(width // tile,),
                in_specs=[
                    pl.BlockSpec((ring, total, tile), lambda i, *_: (0, 0, i + col // tile))
                    for _ in pieces
                ],
                out_specs=pl.BlockSpec((*shape, tile), lambda i, *_: (0, 0, 0, 0, i)),
            ),
            out_shape=jax.ShapeDtypeStruct((*shape, width), pieces[0].dtype),
            compiler_params=pltpu.CompilerParams(vmem_limit_bytes=VMEM_LIMIT),
            cost_estimate=pl.CostEstimate(
                flops=0, bytes_accessed=4 * math.prod(shape) * width, transcendentals=0
            ),
        )(jnp.stack([place.seq, place.core]).astype(jnp.int32), *pieces)
        return whole.reshape(math.prod(shape), width)


def add_low(*terms):
    return sum(t.astype(jnp.float32) for t in terms).astype(jnp.bfloat16)


class Scatter:
    def __init__(self, place, *pairs):
        self.place = place
        self.pairs = []
        theirs = []
        for inputs, deltas in pairs:
            half = deltas.shape[1] // 2
            low, high = deltas[:, :half], deltas[:, half:]
            self.pairs.append((inputs, jnp.where(place.core == 0, low, high)))
            theirs.append(matmul(inputs.T, jnp.where(place.core == 0, high, low)))
        self.theirs = self.side_by_side(theirs)
        self.half = self.theirs.shape[1]
        rows = place.seq_count * place.win_count * place.shard_rows
        self.rounds = self.theirs.shape[0] // rows
        self.seq_rows = rows // place.seq_count

    def side_by_side(self, parts):
        parts = [p.astype(jnp.bfloat16) for p in parts]
        return parts[0] if len(parts) == 1 else jnp.concatenate(parts, axis=1)

    def cores(self):
        def take(passed):
            sums, at = [], 0
            for inputs, mine in self.pairs:
                size = mine.shape[1]
                sums.append(
                    matmul(inputs.T, mine) + passed[:, at : at + size].astype(jnp.float32)
                )
                at += size
            self.sums = self.side_by_side(sums)
            self.blocks = self.sums.reshape(
                self.rounds, self.place.seq_count, self.seq_rows, self.half
            )

        return ((self.theirs,), (self.place.other_core,), take)

    def block(self, m):
        return lax.dynamic_index_in_dim(self.blocks, self.place.seq ^ m, 1, keepdims=False)

    def far(self):
        place, cut = self.place, self.half // 2
        if place.seq_count != 4:
            return ((), (), lambda: None)
        far = self.block(3)

        def take(by_two, by_one):
            one, two = self.block(1), self.block(2)
            self.one = jnp.concatenate([add_low(one[..., :cut], by_two), one[..., cut:]], axis=-1)
            self.two = jnp.concatenate([two[..., :cut], add_low(two[..., cut:], by_one)], axis=-1)

        return (
            (far[..., :cut], far[..., cut:]),
            (lambda v: place.across(v, 2), lambda v: place.across(v, 1)),
            take,
        )

    def near(self):
        place = self.place
        if place.seq_count != 4:
            blocks = [self.block(m) for m in range(place.seq_count)]
            for bit in bits_of(place.seq_count)[::-1]:
                blocks = [
                    add_low(blocks[m], place.across(blocks[m ^ bit], bit)) for m in range(bit)
                ]
            self.kept = [blocks[0]]
            return ((), (), lambda: None)

        def take(one, two):
            self.kept = [self.block(0), one, two]

        return (
            (self.one, self.two),
            (lambda v: place.across(v, 1), lambda v: place.across(v, 2)),
            take,
        )

    def reduced(self):
        ring = self.place.ring
        total = add_low(*self.kept).reshape(self.rounds, ring, self.seq_rows // ring, self.half)
        return [total[i] for i in range(self.rounds)]


class Stack:
    def __init__(self, place, groups, earlier):
        self.place = place
        blocks = [block for group in groups for block in group.reduced()]
        self.lane = math.gcd(*[b.shape[2] for b in blocks])
        self.counts = [b.shape[2] // self.lane for b in blocks]
        self.rows = [b.shape[1] for b in blocks]
        cut = [
            b[:, :, i * self.lane : (i + 1) * self.lane]
            for b, count in zip(blocks, self.counts)
            for i in range(count)
        ]
        self.total = place.sum_to_chips(tie([jnp.concatenate(cut, axis=1)], earlier)[0])

    def finish(self):
        place, at = self.place, 0
        own, send = [], []
        for rows, count in zip(self.rows, self.counts):
            for _ in range(count):
                upper = self.total[at : at + rows // 2]
                lower = self.total[at + rows // 2 : at + rows]
                at += rows
                own.append(jnp.where(place.core == 0, upper, lower))
                send.append(jnp.where(place.core == 0, lower, upper))

        def take(passed):
            self.results, at, number = [], 0, 0
            for rows, count in zip(self.rows, self.counts):
                mine = jnp.concatenate(own[number : number + count], axis=1)
                number += count
                theirs = []
                for _ in range(count):
                    theirs.append(passed[at : at + rows // 2])
                    at += rows // 2
                theirs = jnp.concatenate(theirs, axis=1)
                first = jnp.where(place.core == 0, mine, theirs)
                second = jnp.where(place.core == 0, theirs, mine)
                self.results.append(
                    jnp.concatenate([first, second], axis=1).astype(jnp.float32)
                )

        return ((jnp.concatenate(send, axis=0),), (place.other_core,), take)


VMEM_LIMIT = 56 * 1024 * 1024


def up_to(value, step):
    return -(-value // step) * step


def dot_last(left, right):
    return lax.dot_general(left, right, (((1,), (1,)), ((), ())), preferred_element_type=jnp.float32)


def dot_plain(left, right):
    return jnp.dot(left, right, preferred_element_type=jnp.float32)


def head_lanes(head, width, total):
    return head * width // 128 * 128, min(up_to((head + 1) * width, 128), total)


def keep_lanes(block, first, low, high):
    lane = lax.broadcasted_iota(jnp.int32, block.shape, 1) + first
    return jnp.where((lane >= low) & (lane < high), block, jnp.zeros_like(block))


def window_width(length, bins):
    return up_to(length + bins + (0 if bins % 128 == 0 else 128), 128)


def window_start(length, bins, here):
    base = length - (here + 1) * bins
    if bins % 128 == 0:
        return pl.multiple_of(base, 128), 0
    start = pl.multiple_of(base // 128 * 128, 128)
    return start, base - start


def attend_kernel(sizes, where_ref, *refs):
    blocks, bins, heads, key_size, value_size, wide = sizes
    length = blocks * bins
    kw, vw = heads * key_size, heads * value_size
    pieces, rel_ref = refs[:blocks], refs[blocks]
    outs, probs_ref, keys, values = refs[blocks + 1 : 2 * blocks + 1], *refs[2 * blocks + 1 :]
    step = pl.program_id(0)
    place = where_ref[0]

    @pl.when(step == 0)
    def _():
        for m in range(blocks):
            rows = pl.ds(pl.multiple_of((place ^ m) * bins, bins), bins)
            keys[rows, :] = pieces[m][:, 2 * kw : 3 * kw]
            values[rows, :] = pieces[m][:, 3 * kw :]

    def one(m):
        here = place ^ m
        base, moved = window_start(length, bins, here)
        window = rel_ref[pl.ds(base, wide), :]
        for head in range(heads):
            low, high = head * key_size, (head + 1) * key_size
            q_content = keep_lanes(pieces[m][:, :kw], 0, low, high)
            q_position = keep_lanes(pieces[m][:, kw : 2 * kw], 0, low, high)
            relative = dot_last(q_position, window)
            relative = pltpu.roll(relative, wide - (bins - 1), 1, stride=1, stride_axis=0)
            if bins % 128:
                relative = pltpu.roll(relative, wide - moved, 1)
            scores = dot_last(q_content, keys[...]) + relative[:, :length]
            top = jnp.max(scores, -1, keepdims=True)
            expo = jnp.exp(scores - top)
            probs = (expo * (1.0 / jnp.sum(expo, -1, keepdims=True))).astype(jnp.bfloat16)
            probs_ref[0, head] = probs
            first, last = head_lanes(head, value_size, vw)
            mixed = dot_plain(probs, values[:, first:last])
            mixed = keep_lanes(mixed, first, head * value_size, (head + 1) * value_size)
            if head == 0:
                outs[m][...] = jnp.zeros_like(outs[m])
            outs[m][:, first:last] += mixed.astype(jnp.bfloat16)

    for m in range(blocks):
        pl.when(step == m)(functools.partial(one, m))


def attend(pieces, rel_keys, place, heads, key_size, value_size):
    blocks, bins = len(pieces), pieces[0].shape[0]
    length = blocks * bins
    wide = window_width(length, bins)
    kw, vw = heads * key_size, heads * value_size
    whole = lambda shape: pl.BlockSpec(shape, lambda i, *_: (0,) * len(shape))
    sizes = (blocks, bins, heads, key_size, value_size, wide)
    flops = 2 * heads * length * length * (2 * key_size + value_size)
    result = pl.pallas_call(
        functools.partial(attend_kernel, sizes),
        grid_spec=pltpu.PrefetchScalarGridSpec(
            num_scalar_prefetch=1,
            grid=(blocks,),
            in_specs=[whole(p.shape) for p in pieces] + [whole(rel_keys.shape)],
            out_specs=[whole((bins, vw))] * blocks
            + [pl.BlockSpec((1, heads, bins, length), lambda i, *_: (i, 0, 0, 0))],
            scratch_shapes=[
                pltpu.VMEM((length, kw), jnp.bfloat16),
                pltpu.VMEM((length, vw), jnp.bfloat16),
            ],
        ),
        out_shape=[jax.ShapeDtypeStruct((bins, vw), jnp.bfloat16)] * blocks
        + [jax.ShapeDtypeStruct((blocks, heads, bins, length), jnp.bfloat16)],
        compiler_params=pltpu.CompilerParams(vmem_limit_bytes=VMEM_LIMIT),
        cost_estimate=pl.CostEstimate(
            flops=flops * 2, bytes_accessed=2 * heads * length * length, transcendentals=heads * length * length
        ),
    )(place, *pieces, rel_keys)
    return result[:blocks], result[blocks]


def attend_back_kernel(sizes, where_ref, *refs):
    blocks, bins, heads, key_size, value_size, wide = sizes
    length = blocks * bins
    kw, vw = heads * key_size, heads * value_size
    key_scale = key_size ** (-0.5)
    pieces, grads, rel_ref, probs_ref = (
        refs[:blocks], refs[blocks : 2 * blocks], refs[2 * blocks], refs[2 * blocks + 1],
    )
    rest = refs[2 * blocks + 2 :]
    outs, rel_grad, sums, keys, values, key_grad, value_grad = rest[:blocks], *rest[blocks:]
    step = pl.program_id(0)
    place = where_ref[0]

    @pl.when(step == 0)
    def _():
        for m in range(blocks):
            rows = pl.ds(pl.multiple_of((place ^ m) * bins, bins), bins)
            keys[rows, :] = pieces[m][:, 2 * kw : 3 * kw]
            values[rows, :] = pieces[m][:, 3 * kw :]
        rel_grad[...] = jnp.zeros_like(rel_grad)
        sums[...] = jnp.zeros_like(sums)
        key_grad[...] = jnp.zeros_like(key_grad)
        value_grad[...] = jnp.zeros_like(value_grad)

    def one(m):
        here = place ^ m
        base, moved = window_start(length, bins, here)
        window = rel_ref[pl.ds(base, wide), :]
        total = None
        row = lax.broadcasted_iota(jnp.int32, (bins, bins), 0)
        col = lax.broadcasted_iota(jnp.int32, (bins, bins), 1)
        flip = jnp.where(row + col == bins - 1, 1.0, 0.0).astype(jnp.bfloat16)
        for head in range(heads):
            low, high = head * key_size, (head + 1) * key_size
            vlow, vhigh = head * value_size, (head + 1) * value_size
            first, last = head_lanes(head, value_size, vw)
            probs = probs_ref[0, head]
            out_grad = keep_lanes(grads[m][:, first:last], first, vlow, vhigh)
            prob_grad = dot_last(out_grad, values[:, first:last])
            probs_f = probs.astype(jnp.float32)
            row_delta = jnp.sum(probs_f * prob_grad, -1, keepdims=True)
            delta = (probs_f * (prob_grad - row_delta)).astype(jnp.bfloat16)
            value_grad[first:last, :] += dot_plain(out_grad.T, probs)
            q_content = keep_lanes(pieces[m][:, :kw], 0, low, high)
            q_position = keep_lanes(pieces[m][:, kw : 2 * kw], 0, low, high)
            key_grad[...] += dot_plain(q_content.T, delta)
            content = keep_lanes(dot_plain(delta, keys[...]), 0, low, high)
            shifted = jnp.concatenate(
                [dot_plain(flip, delta), jnp.zeros((bins, wide - length), jnp.float32)], axis=1
            )
            shifted = pltpu.roll(shifted, 0, 1, stride=1, stride_axis=0)
            if bins % 128:
                shifted = pltpu.roll(shifted, moved, 1)
            shifted = shifted.astype(jnp.bfloat16)
            position = keep_lanes(dot_plain(shifted, window), 0, low, high)
            position = jnp.dot(
                flip.astype(jnp.float32),
                position,
                precision=lax.Precision.HIGHEST,
                preferred_element_type=jnp.float32,
            )
            q_position = dot_plain(flip, q_position).astype(jnp.bfloat16)
            rel_grad[:, pl.ds(base, wide)] += dot_plain(q_position.T, shifted)
            sums[0:1, :] += jnp.sum(content, 0, keepdims=True)
            sums[1:2, :] += jnp.sum(position, 0, keepdims=True)
            both = content + position
            total = both if total is None else total + both
        outs[m][:, :kw] = (total * key_scale).astype(jnp.bfloat16)

    for m in range(blocks):
        pl.when(step == m)(functools.partial(one, m))

    @pl.when(step == blocks - 1)
    def _():
        keys[...] = key_grad[...].T.astype(jnp.bfloat16)
        values[...] = value_grad[...].T.astype(jnp.bfloat16)
        for m in range(blocks):
            rows = pl.ds(pl.multiple_of((place ^ m) * bins, bins), bins)
            outs[m][:, kw : 2 * kw] = keys[rows, :]
            outs[m][:, 2 * kw :] = values[rows, :]


def attend_back(pieces, grads, rel_keys, probs, place, heads, key_size, value_size):
    blocks, bins = len(pieces), pieces[0].shape[0]
    length = blocks * bins
    wide = window_width(length, bins)
    kw, vw = heads * key_size, heads * value_size
    whole = lambda shape: pl.BlockSpec(shape, lambda i, *_: (0,) * len(shape))
    sizes = (blocks, bins, heads, key_size, value_size, wide)
    rel_shape = (kw, rel_keys.shape[0])
    flops = 2 * heads * length * length * (4 * key_size + 2 * value_size)
    result = pl.pallas_call(
        functools.partial(attend_back_kernel, sizes),
        grid_spec=pltpu.PrefetchScalarGridSpec(
            num_scalar_prefetch=1,
            grid=(blocks,),
            in_specs=[whole(p.shape) for p in pieces]
            + [whole(g.shape) for g in grads]
            + [whole(rel_keys.shape)]
            + [pl.BlockSpec((1, heads, bins, length), lambda i, *_: (i, 0, 0, 0))],
            out_specs=[whole((bins, 2 * kw + vw))] * blocks + [whole(rel_shape), whole((8, kw))],
            scratch_shapes=[
                pltpu.VMEM((length, kw), jnp.bfloat16),
                pltpu.VMEM((length, vw), jnp.bfloat16),
                pltpu.VMEM((kw, length), jnp.float32),
                pltpu.VMEM((vw, length), jnp.float32),
            ],
        ),
        out_shape=[jax.ShapeDtypeStruct((bins, 2 * kw + vw), jnp.bfloat16)] * blocks
        + [jax.ShapeDtypeStruct(rel_shape, jnp.float32), jax.ShapeDtypeStruct((8, kw), jnp.float32)],
        compiler_params=pltpu.CompilerParams(vmem_limit_bytes=VMEM_LIMIT),
        cost_estimate=pl.CostEstimate(
            flops=flops * 2, bytes_accessed=2 * heads * length * length, transcendentals=0
        ),
    )(place, *pieces, *grads, rel_keys, probs)
    return result[:blocks], result[blocks], result[blocks + 1]


def heads_kernel(sizes, where_ref, layer, weight, bias, human, mouse, out_grad, grad, bias_grad, turned):
    tile, human_tiles, human_tracks, mouse_tracks = sizes
    step = pl.program_id(0)
    species, first, last = where_ref[0], where_ref[1], where_ref[2]
    is_human = step < human_tiles

    @pl.when(step == 0)
    def _():
        turned[...] = layer[...].T
        grad[...] = jnp.zeros_like(grad)

    wanted = jnp.where(is_human, 0, 1) == species

    def one(cotangent, start, tracks):
        logit = dot_plain(layer[...], weight[...]) + bias[...]
        row = lax.broadcasted_iota(jnp.int32, logit.shape, 0)
        col = lax.broadcasted_iota(jnp.int32, logit.shape, 1) + start
        inside = (row >= first) & (row < last) & (col < tracks)
        scale = cotangent[...].astype(jnp.float32) * (1.0 / (1.0 + jnp.exp(-logit)))
        delta_f = jnp.where(inside, scale, 0.0)
        delta = delta_f.astype(jnp.bfloat16)
        bias_grad[...] = jnp.sum(delta.astype(jnp.float32), 0, keepdims=True)
        out_grad[...] = dot_plain(turned[...], delta).astype(jnp.bfloat16)
        grad[...] += dot_last(delta, weight[...])

    @pl.when(wanted & is_human)
    def _():
        one(human, step * tile, human_tracks)

    @pl.when(wanted & jnp.logical_not(is_human))
    def _():
        one(mouse, (step - human_tiles) * tile, mouse_tracks)

    @pl.when(jnp.logical_not(wanted))
    def _():
        out_grad[...] = jnp.zeros_like(out_grad)
        bias_grad[...] = jnp.zeros_like(bias_grad)


def both_heads(layer, weight, first, bias, human, mouse, where, tile):
    rows, width = layer.shape
    human_tiles = -(-human.shape[1] // tile)
    mouse_tiles = -(-mouse.shape[1] // tile)
    tiles = human_tiles + mouse_tiles
    sizes = (tile, human_tiles, human.shape[1], mouse.shape[1])
    return pl.pallas_call(
        functools.partial(heads_kernel, sizes),
        grid_spec=pltpu.PrefetchScalarGridSpec(
            num_scalar_prefetch=1,
            grid=(tiles,),
            in_specs=[
                pl.BlockSpec((rows, width), lambda i, *_: (0, 0)),
                pl.BlockSpec((width, tile), lambda i, *_: (0, first // tile + i)),
                pl.BlockSpec((1, tile), lambda i, *_: (0, i)),
                pl.BlockSpec((rows, tile), lambda i, *_: (0, jnp.minimum(i, human_tiles - 1))),
                pl.BlockSpec((rows, tile), lambda i, *_: (0, jnp.maximum(i - human_tiles, 0))),
            ],
            out_specs=[
                pl.BlockSpec((width, tile), lambda i, *_: (0, i)),
                pl.BlockSpec((rows, width), lambda i, *_: (0, 0)),
                pl.BlockSpec((1, tile), lambda i, *_: (0, i)),
            ],
            scratch_shapes=[pltpu.VMEM((width, rows), jnp.bfloat16)],
        ),
        out_shape=[
            jax.ShapeDtypeStruct((width, tiles * tile), jnp.bfloat16),
            jax.ShapeDtypeStruct((rows, width), jnp.float32),
            jax.ShapeDtypeStruct((1, tiles * tile), jnp.float32),
        ],
        compiler_params=pltpu.CompilerParams(vmem_limit_bytes=VMEM_LIMIT),
        cost_estimate=pl.CostEstimate(
            flops=6 * rows * width * tiles * tile,
            bytes_accessed=4 * width * tiles * tile,
            transcendentals=rows * tiles * tile,
        ),
    )(where, layer, weight, bias, human, mouse)


def feed_kernel(rounds, inputs, up, bias, down, resid, out_bias, hidden_out, middle_out, out, total):
    step, count = pl.program_id(0), pl.num_programs(0)
    hidden = dot_plain(inputs[...], up[...]) + bias[...]
    hidden_out[...] = hidden
    middle = (hidden * (1.0 / (1.0 + jnp.exp(-1.702 * hidden)))).astype(jnp.bfloat16)
    middle_out[...] = middle
    part = dot_plain(middle, down[...])

    @pl.when(step == 0)
    def _():
        total[...] = resid[...] + out_bias[...] + part

    @pl.when(step > 0)
    def _():
        total[...] += part

    @pl.when(step == count - 1)
    def _():
        out[...] = total[...].astype(jnp.bfloat16)


def feed_back_kernel(out_delta, hidden, down, up, delta_out, bias_grad, grad):
    @pl.when(pl.program_id(0) == 0)
    def _():
        grad[...] = jnp.zeros_like(grad)

    middle_grad = dot_last(out_delta[...], down[...])
    gated = 1.0 / (1.0 + jnp.exp(-1.702 * hidden[...]))
    delta = middle_grad * (gated + 1.702 * hidden[...] * gated * (1.0 - gated))
    delta = delta.astype(jnp.bfloat16)
    delta_out[...] = delta
    bias_grad[...] = jnp.sum(delta.astype(jnp.float32), 0, keepdims=True)
    grad[...] += dot_last(delta, up[...])


class Feed:
    def __init__(self, late, width, hidden_width, tile):
        self.late, self.width, self.hidden_width, self.tile = late, width, hidden_width, tile
        self.rounds = hidden_width // width
        each, skip = width // tile, hidden_width // tile
        self.up = pl.BlockSpec((width, tile), lambda i: (0, skip + i))
        self.down = pl.BlockSpec((tile, width), lambda i: (i % each, i // each))
        self.params = pltpu.CompilerParams(vmem_limit_bytes=VMEM_LIMIT)

    def cost(self, rows):
        return pl.CostEstimate(
            flops=4 * rows * self.width * self.hidden_width,
            bytes_accessed=4 * self.width * self.hidden_width,
            transcendentals=rows * self.hidden_width,
        )

    def forward(self, inputs, bias, resid, out_bias):
        rows = inputs.shape[0]
        full = lambda r: pl.BlockSpec((r, self.width), lambda i: (0, 0))
        some = lambda r: pl.BlockSpec((r, self.tile), lambda i: (0, i))
        return pl.pallas_call(
            functools.partial(feed_kernel, self.rounds),
            grid=(self.hidden_width // self.tile,),
            in_specs=[full(rows), self.up, some(1), self.down, full(rows), full(1)],
            out_specs=[some(rows), some(rows), full(rows)],
            out_shape=[
                jax.ShapeDtypeStruct((rows, self.hidden_width), jnp.float32),
                jax.ShapeDtypeStruct((rows, self.hidden_width), jnp.bfloat16),
                jax.ShapeDtypeStruct((rows, self.width), jnp.bfloat16),
            ],
            scratch_shapes=[pltpu.VMEM((rows, self.width), jnp.float32)],
            compiler_params=self.params,
            cost_estimate=self.cost(rows),
        )(inputs, self.late, bias[None], self.late, resid, out_bias[None])

    def back(self, out_delta, hidden):
        rows = out_delta.shape[0]
        full = pl.BlockSpec((rows, self.width), lambda i: (0, 0))
        some = lambda r: pl.BlockSpec((r, self.tile), lambda i: (0, i))
        return pl.pallas_call(
            feed_back_kernel,
            grid=(self.hidden_width // self.tile,),
            in_specs=[full, some(rows), self.down, self.up],
            out_specs=[some(rows), some(1), full],
            out_shape=[
                jax.ShapeDtypeStruct((rows, self.hidden_width), jnp.bfloat16),
                jax.ShapeDtypeStruct((1, self.hidden_width), jnp.float32),
                jax.ShapeDtypeStruct((rows, self.width), jnp.float32),
            ],
            compiler_params=self.params,
            cost_estimate=self.cost(rows),
        )(out_delta, hidden, self.late, self.late)


def shards(
    features,
    species,
    crop_start,
    human_grad,
    mouse_grad,
    batch_gain,
    batch_bias,
    first_gain,
    first_bias,
    w_query,
    w_key,
    w_value,
    w_position,
    content_bias,
    position_bias,
    w_out,
    b_out,
    second_gain,
    second_bias,
    w_up,
    b_up,
    w_down,
    b_down,
    w_human,
    b_human,
    w_mouse,
    b_mouse,
):
    place = Place(w_query.shape[0])
    seq_count = place.seq_count
    windows, bin_count, model_width = features.shape
    assert windows == 1
    head_count, key_size = content_bias.shape
    value_size = model_width // head_count
    length = bin_count * seq_count
    token_total = bin_count * seq_count * place.win_count
    key_scale = key_size ** (-0.5)
    heads = head_count // seq_count
    kw, vw = heads * key_size, heads * value_size
    human_tracks, mouse_tracks = b_human.shape[0], b_mouse.shape[0]
    tile = 896
    human_wide, mouse_wide = up_to(human_tracks, tile), up_to(mouse_tracks, tile)
    tracks = human_wide + mouse_wide

    def side_by_side(human, mouse):
        return jnp.concatenate(
            [
                jnp.pad(human, [(0, 0)] * (human.ndim - 1) + [(0, human_wide - human_tracks)]),
                jnp.pad(mouse, [(0, 0)] * (mouse.ndim - 1) + [(0, mouse_wide - mouse_tracks)]),
            ],
            axis=-1,
        )

    shard_rows = w_query.shape[0]
    attn_shard = jnp.concatenate(
        [
            w_query.reshape(shard_rows, seq_count, kw),
            w_key.reshape(shard_rows, seq_count, kw),
            w_value.reshape(shard_rows, seq_count, vw),
        ],
        axis=2,
    ).reshape(shard_rows, -1)
    head_shard = side_by_side(w_human, w_mouse)
    attn_width, up_width = attn_shard.shape[1], w_up.shape[1]
    devices = seq_count * place.win_count
    rounds = w_down.shape[0] // shard_rows

    def to_rounds(value):
        split = value.reshape(*value.shape[:-1], devices, rounds, shard_rows)
        return jnp.swapaxes(split, -3, -2).reshape(value.shape)

    def from_rounds(value):
        split = value.reshape(*value.shape[:-1], rounds, devices, shard_rows)
        return jnp.swapaxes(split, -3, -2).reshape(value.shape)

    down_parts = [w_down[i * shard_rows : (i + 1) * shard_rows] for i in range(rounds)]
    head_at = up_to(2 * up_width, tile)
    gap = jnp.zeros((shard_rows, head_at - 2 * up_width), jnp.bfloat16)
    late_shard = jnp.concatenate([*down_parts, to_rounds(w_up), gap, head_shard], axis=1)
    late_full = lax.all_gather(late_shard, ("seq", "win"), axis=0, tiled=True)
    feed = Feed(late_full, model_width, up_width, math.gcd(model_width, 512))
    steps = Steps()
    first_w = Gather(place, jnp.concatenate([attn_shard, w_out], axis=1))
    steps.run(first_w.ring_first())
    steps.run(first_w.ring_last())
    flat_in = features.astype(jnp.float32).reshape(bin_count, model_width)
    channel_sum, square_sum = place.total(
        jnp.stack([jnp.sum(flat_in, 0), jnp.sum(flat_in * flat_in, 0)])
    )
    channel_mean = channel_sum / token_total
    inv_std = lax.rsqrt(square_sum / token_total - channel_mean * channel_mean + 1e-05)
    batch_hat = (flat_in - channel_mean) * inv_std
    normed = batch_hat * batch_gain + batch_bias
    first_hat, first_scale = norm_parts(normed)
    attn_in = (first_hat * first_gain + first_bias).astype(jnp.bfloat16)

    wide = window_width(length, bin_count)
    distance = (jnp.arange(length + wide) - (length - 1)).astype(jnp.float32)
    basis_low = position_basis(distance, w_position.shape[0], length).astype(jnp.bfloat16)
    position_mine = lax.dynamic_slice_in_dim(w_position, place.seq * kw, kw, 1)
    rel_keys = matmul(basis_low, position_mine).astype(jnp.bfloat16)

    steps.run(first_w.near())
    steps.before.append(attn_in)
    steps.run(first_w.far(), first_w.core_first())
    steps.run(first_w.core_last())
    attn_full = first_w.whole(0, shard_rows, 0, attn_width)
    out_full = first_w.whole(0, shard_rows, attn_width, model_width)
    mixed = matmul(attn_in, attn_full)
    group = 2 * kw + vw
    packed = []
    for g in range(seq_count):
        queries = mixed[:, g * group : g * group + kw] * key_scale
        heads_at = slice(g * heads, (g + 1) * heads)
        packed.append(
            jnp.concatenate(
                [
                    (queries + content_bias[heads_at].reshape(kw)).astype(jnp.bfloat16),
                    (queries + position_bias[heads_at].reshape(kw)).astype(jnp.bfloat16),
                    mixed[:, g * group + kw : (g + 1) * group].astype(jnp.bfloat16),
                ],
                axis=1,
            )
        )

    def swap(pieces):
        results = list(pieces[:1])
        moves = [functools.partial(place.across, bits=m) for m in range(1, seq_count)]
        return (pieces[1:], moves, lambda *came: results.extend(came)), results

    job, pieces = swap(place.by_seq(packed))
    steps.run(job)
    spot = place.seq.astype(jnp.int32).reshape(1)
    mixed_pieces, probs = attend(pieces, rel_keys, spot, heads, key_size, value_size)
    job, mixed_pieces = swap(mixed_pieces)
    steps.run(job)
    attended = jnp.concatenate(place.by_seq(mixed_pieces), axis=1)
    resid = normed + matmul(attended, out_full) + b_out
    second_hat, second_scale = norm_parts(resid)
    mlp_in = (second_hat * second_gain + second_bias).astype(jnp.bfloat16)
    hidden, middle, layer_low = feed.forward(mlp_in, to_rounds(b_up), resid, b_down)
    first_row = crop_start[0] - place.seq * bin_count
    head_grad, layer_grad, head_bias_grad = both_heads(
        layer_low,
        late_full,
        head_at,
        side_by_side(b_human, b_mouse)[None],
        human_grad.reshape(bin_count, human_tracks),
        mouse_grad.reshape(bin_count, mouse_tracks),
        jnp.stack([species[0], first_row, first_row + CROP]).astype(jnp.int32),
        tile,
    )
    head_bias_grad = head_bias_grad[0]
    head_rows = lax.psum_scatter(head_grad, ("seq", "win"), scatter_dimension=0, tiled=True)
    down_delta = layer_grad.astype(jnp.bfloat16)
    down = Scatter(place, (middle, down_delta))
    steps.run(down.cores())
    down_bias_grad = jnp.sum(down_delta.astype(jnp.float32), 0)
    hidden_delta, up_bias_grad, mlp_in_grad = feed.back(down_delta, hidden)
    up_bias_grad = up_bias_grad[0]
    up = Scatter(place, (mlp_in, hidden_delta))
    steps.run(down.far(), up.cores())
    resid_grad, second_gain_grad, second_bias_grad = norm_back(
        layer_grad, mlp_in_grad, second_hat, second_scale, second_gain
    )
    out_delta = resid_grad.astype(jnp.bfloat16)
    out = Scatter(place, (attended, out_delta))
    out_bias_grad = jnp.sum(out_delta.astype(jnp.float32), 0)
    attended_delta = matmul(out_delta, out_full.T).astype(jnp.bfloat16)
    job, grads = swap(
        place.by_seq([attended_delta[:, g * vw : (g + 1) * vw] for g in range(seq_count)])
    )
    steps.run(job)
    steps.run(down.near(), up.far(), out.cores())
    delta_pieces, rel_grad, head_sums = attend_back(
        pieces, grads, rel_keys, probs, spot, heads, key_size, value_size
    )
    *delta_pieces, rel_grad, head_sums = steps.hold(*delta_pieces, rel_grad, head_sums)
    job, delta_pieces = swap(delta_pieces)
    steps.run(job, up.near())
    first_stack = Stack(place, (down, up), [head_rows])
    attn_delta = jnp.concatenate(place.by_seq(delta_pieces), axis=1)
    attn = Scatter(place, (attn_in, attn_delta))
    steps.run(out.far(), attn.cores())
    steps.run(out.near(), attn.far())
    steps.run(attn.near())
    second_stack = Stack(place, (out, attn), [first_stack.total])
    steps.run(first_stack.finish())
    steps.run(second_stack.finish())
    *down_rows, up_rows = first_stack.results
    down_rows = jnp.concatenate(down_rows, axis=0)
    up_rows = from_rounds(up_rows)
    out_rows, attn_rows = second_stack.results
    head_rows = head_rows.astype(jnp.float32)
    attn_grad = matmul(attn_delta, attn_full.T)
    normed_grad, first_gain_grad, first_bias_grad = norm_back(
        resid_grad, attn_grad, first_hat, first_scale, first_gain
    )

    position_weight_grad = lax.dot_general(
        rel_grad,
        basis_low.astype(jnp.float32),
        (((1,), (0,)), ((), ())),
        precision=lax.Precision.HIGHEST,
        preferred_element_type=jnp.float32,
    )
    per_head = place.total(
        jnp.concatenate([position_weight_grad, head_sums[:2].T], axis=1), over_seq=False
    )
    per_head = [per_head] + [place.across(per_head, m) for m in range(1, seq_count)]
    per_head = jnp.concatenate(place.by_seq(per_head), axis=0)
    features_count = w_position.shape[0]
    position_total = per_head[:, :features_count].T
    content_total = per_head[:, features_count].reshape(head_count, key_size)
    position_bias_total = per_head[:, features_count + 1].reshape(head_count, key_size)

    parts = [
        jnp.sum(normed_grad * batch_hat, 0),
        jnp.sum(normed_grad, 0),
        first_gain_grad,
        first_bias_grad,
        head_bias_grad[:human_tracks],
        head_bias_grad[human_wide : human_wide + mouse_tracks],
        down_bias_grad,
        up_bias_grad,
        second_gain_grad,
        second_bias_grad,
        out_bias_grad,
    ]
    ends = [0]
    for part in parts:
        ends.append(ends[-1] + up_to(part.shape[0], 1024))
    totals = place.total(
        jnp.concatenate([jnp.pad(p, (0, up_to(p.shape[0], 1024) - p.shape[0])) for p in parts])
    )
    (
        batch_gain_total,
        batch_bias_total,
        first_gain_total,
        first_bias_total,
        human_bias_total,
        mouse_bias_total,
        down_bias_total,
        up_bias_total,
        second_gain_total,
        second_bias_total,
        out_bias_total,
    ) = [totals[at : at + p.shape[0]] for at, p in zip(ends, parts)]
    scaled_grad = normed_grad * batch_gain
    input_grad = inv_std * (
        scaled_grad
        - batch_gain * batch_bias_total / token_total
        - batch_hat * batch_gain * batch_gain_total / token_total
    )
    attn_rows = attn_rows.reshape(shard_rows, seq_count, 2 * kw + vw)
    return (
        layer_low.reshape(windows, bin_count, model_width),
        input_grad.astype(jnp.bfloat16).reshape(windows, bin_count, model_width),
        batch_gain_total,
        batch_bias_total,
        first_gain_total,
        first_bias_total,
        attn_rows[:, :, :kw].reshape(shard_rows, -1),
        attn_rows[:, :, kw : 2 * kw].reshape(shard_rows, -1),
        attn_rows[:, :, 2 * kw :].reshape(shard_rows, -1),
        position_total,
        content_total,
        position_bias_total,
        out_rows,
        out_bias_total,
        second_gain_total,
        second_bias_total,
        up_rows,
        from_rounds(up_bias_total),
        down_rows,
        down_bias_total,
        head_rows[:, :human_tracks],
        human_bias_total,
        head_rows[:, human_wide : human_wide + mouse_tracks],
        mouse_bias_total,
    )


def solution(mesh):
    in_specs = (
        P("win", "seq", None),
        P("win"),
        P("win"),
        P("win", "seq", None),
        P("win", "seq", None),
        P(),
        P(),
        P(),
        P(),
        P(("seq", "win"), None),
        P(("seq", "win"), None),
        P(("seq", "win"), None),
        P(),
        P(),
        P(),
        P(("seq", "win"), None),
        P(),
        P(),
        P(),
        P(("seq", "win"), None),
        P(),
        P(("seq", "win"), None),
        P(),
        P(("seq", "win"), None),
        P(),
        P(("seq", "win"), None),
        P(),
    )
    out_specs = (
        P("win", "seq", None),
        P("win", "seq", None),
        P(),
        P(),
        P(),
        P(),
        P(("seq", "win"), None),
        P(("seq", "win"), None),
        P(("seq", "win"), None),
        P(),
        P(),
        P(),
        P(("seq", "win"), None),
        P(),
        P(),
        P(),
        P(("seq", "win"), None),
        P(),
        P(("seq", "win"), None),
        P(),
        P(("seq", "win"), None),
        P(),
        P(("seq", "win"), None),
        P(),
    )
    return jax.shard_map(shards, mesh=mesh, in_specs=in_specs, out_specs=out_specs, check_vma=False)
```
